128 devices in a mesh: section: 2 (over x_lo), dp: 16 (over x_hi, z, core), tensor: 4 (over y).
Axes of the slice: x: 4 (x_hi: 2, x_lo: 2; x = x_hi * 2 + x_lo), y: 4, z: 4, core: 2. Of those that a mesh axis runs over, the one named last changes fastest.
Arguments:
- stream_in: bfloat16 [32, 640, 1024], P('dp', 'tensor'), may hold values from -6 to 6
- cotangent: bfloat16 [32, 640, 1024], P('dp', 'tensor'), may hold values from -6 to 6
- mixer_gain: bfloat16 [2, 1024], P('section'), may hold values from 0.5 to 1.5
- mamba_in: bfloat16 [2, 1024, 2, 1536], P('section', None, None, 'tensor'), may hold values from -0.1875 to 0.1875
- state_in: bfloat16 [2, 1024, 256], P('section'), may hold values from -0.1875 to 0.1875
- step_in: bfloat16 [2, 1024, 24], P('section', None, 'tensor'), may hold values from -0.1875 to 0.1875
- mamba_conv: bfloat16 [2, 4, 1536], P('section', None, 'tensor'), may hold values from -3 to 3
- state_conv: bfloat16 [2, 4, 256], P('section'), may hold values from -3 to 3
- step_bias: float32 [2, 24], P('section', 'tensor'), may hold values from -4 to -1.5
- decay_log: float32 [2, 24], P('section', 'tensor'), may hold values from -1 to 1
- skip_gain: float32 [2, 24], P('section', 'tensor'), may hold values from 0.5 to 1.5
- query_in: bfloat16 [2, 1024, 512], P('section', None, 'tensor'), may hold values from -0.1875 to 0.1875
- keyval_in: bfloat16 [2, 1024, 2, 128], P('section'), may hold values from -0.1875 to 0.1875
- mamba_out: bfloat16 [2, 1536, 1024], P('section', 'tensor'), may hold values from -0.0390625 to 0.0390625
- attention_out: bfloat16 [2, 512, 1024], P('section', 'tensor'), may hold values from -0.5 to 0.5
- feed_gain: bfloat16 [2, 1024], P('section'), may hold values from 0.5 to 1.5
- gate_up: bfloat16 [2, 1024, 2, 2048], P('section', None, None, 'tensor'), may hold values from -0.1875 to 0.1875
- down_weight: bfloat16 [2, 2048, 1024], P('section', 'tensor'), may hold values from -0.125 to 0.125
Outputs:
- section_output: float32 [2, 32, 640, 1024], P('section', 'dp', 'tensor')
- input_grad: float32 [2, 32, 640, 1024], P('section', 'dp', 'tensor')
- grad_mixer_gain: float32 [2, 1024], P('section', ('dp', 'tensor'))
- grad_mamba_in: float32 [2, 1024, 2, 1536], P('section', 'dp', None, 'tensor')
- grad_state_in: float32 [2, 1024, 256], P('section', ('dp', 'tensor'))
- grad_step_in: float32 [2, 1024, 24], P('section', 'dp', 'tensor')
- grad_mamba_conv: float32 [2, 4, 1536], P('section', None, 'tensor')
- grad_state_conv: float32 [2, 4, 256], P('section', None, ('dp', 'tensor'))
- grad_step_bias: float32 [2, 24], P('section', 'tensor')
- grad_decay_log: float32 [2, 24], P('section', 'tensor')
- grad_skip_gain: float32 [2, 24], P('section', 'tensor')
- grad_query_in: float32 [2, 1024, 512], P('section', 'dp', 'tensor')
- grad_keyval_in: float32 [2, 1024, 2, 128], P('section', ('dp', 'tensor'))
- grad_mamba_out: float32 [2, 1536, 1024], P('section', 'tensor', 'dp')
- grad_attention_out: float32 [2, 512, 1024], P('section', 'tensor', 'dp')
- grad_feed_gain: float32 [2, 1024], P('section', ('dp', 'tensor'))
- grad_gate_up: float32 [2, 1024, 2, 2048], P('section', 'dp', None, 'tensor')
- grad_down_weight: float32 [2, 2048, 1024], P('section', 'tensor', 'dp')
The draws below stay inside these ranges and needn't reach their ends.
All inputs are finite; a program needn't handle non-finite values.
Results may differ from the reference program's by a relative error of at most 0.024.
Values may be sent and summed in bfloat16 or wider, within the bound.
A program may use at most 256 MiB of HBM per device.

```python
import jax
import jax.numpy as jnp
from jax import lax

D = 1024
MHEADS = 24
NSTATE = 128
KCONV = 4
HEAD_DIM = 64
FF = 2048
SEQ_LEN = 640
DSSM = 1536
ATT_DIM = 512
KV_DIM = 128
SEQS = 32
N_SECTION = 2


def levels(key, dims, cuts, least, high):
    def one(axis_at, parts):
        draws = jax.random.uniform(jax.random.fold_in(jax.random.fold_in(key, 6), axis_at), (parts,), jnp.float32, least / len(cuts), high / len(cuts))
        return jnp.repeat(jnp.exp(draws), dims[axis_at] // parts).reshape((-1,) + (1,) * (len(dims) - axis_at - 1))

    factor_of = one(*cuts[0])
    for cut in cuts[1:]:
        factor_of = factor_of * one(*cut)
    return factor_of


def bell_draw(key, shape, spread, bound, pieces=(), kind=jnp.bfloat16):
    entries = jax.random.normal(key, shape, jnp.float32) * spread
    if len(pieces) > 0:
        entries = levels(key, shape, pieces, -0.22, 0.18) * entries
    return jnp.clip(entries, min=-bound, max=bound).astype(kind)


def setup_inputs(seed: int = 0) -> dict:
    keys = jax.random.split(jax.random.key(seed), 19)
    stream_in = bell_draw(keys[0], (SEQS, SEQ_LEN, D), 1.0, 6.0, ((0, 16), (1, 4)))
    cotangent = bell_draw(keys[1], (SEQS, SEQ_LEN, D), 1.0, 6.0, ((0, 16), (1, 4)))
    mixer_gain = jnp.clip(1.0 + 0.1 * jax.random.normal(keys[2], (N_SECTION, D), jnp.float32), 0.5, 1.5).astype(jnp.bfloat16)
    mamba_in = bell_draw(keys[3], (N_SECTION, D, 2, DSSM), D ** -0.5, 0.1875, ((0, 2), (3, 4)))
    state_in = bell_draw(keys[4], (N_SECTION, D, 2 * NSTATE), D ** -0.5, 0.1875, ((0, 2),))
    step_in = bell_draw(keys[5], (N_SECTION, D, MHEADS), D ** -0.5, 0.1875, ((0, 2), (2, 4)))
    mamba_conv = bell_draw(keys[6], (N_SECTION, KCONV, DSSM), KCONV ** -0.5, 3.0, ((0, 2), (2, 4)))
    state_conv = bell_draw(keys[7], (N_SECTION, KCONV, 2 * NSTATE), KCONV ** -0.5, 3.0, ((0, 2),))
    step_bias = jnp.clip(-4.0 + 2.5 * jax.random.uniform(keys[8], (N_SECTION, MHEADS), jnp.float32) ** levels(keys[8], (N_SECTION, MHEADS), ((0, 2), (1, 4)), -0.2, 0.2), -4.0, -1.5)
    decay_log = jnp.clip(jax.random.uniform(keys[9], (N_SECTION, MHEADS), jnp.float32, -1.0, 1.0) * levels(keys[9], (N_SECTION, MHEADS), ((0, 2), (1, 4)), -0.4, 0.0), -1.0, 1.0)
    skip_gain = jnp.clip(0.5 + 1.0 * jax.random.uniform(keys[10], (N_SECTION, MHEADS), jnp.float32) ** levels(keys[10], (N_SECTION, MHEADS), ((0, 2), (1, 4)), -0.2, 0.2), 0.5, 1.5)
    query_in = bell_draw(keys[11], (N_SECTION, D, ATT_DIM), D ** -0.5, 0.1875, ((0, 2), (2, 4)))
    keyval_in = bell_draw(keys[12], (N_SECTION, D, 2, KV_DIM), D ** -0.5, 0.1875, ((0, 2),))
    mamba_out = bell_draw(keys[13], (N_SECTION, DSSM, D), (DSSM * NSTATE // 8) ** -0.5, 0.0390625, ((0, 2), (1, 4)))
    attention_out = bell_draw(keys[14], (N_SECTION, ATT_DIM, D), (ATT_DIM // 4) ** -0.5, 0.5, ((0, 2), (1, 4)))
    feed_gain = jnp.clip(1.0 + 0.1 * jax.random.normal(keys[15], (N_SECTION, D), jnp.float32), 0.5, 1.5).astype(jnp.bfloat16)
    gate_up = bell_draw(keys[16], (N_SECTION, D, 2, FF), D ** -0.5, 0.1875, ((0, 2), (3, 4)))
    down_weight = bell_draw(keys[17], (N_SECTION, FF, D), FF ** -0.5, 0.125, ((0, 2), (1, 4)))
    return dict(stream_in=stream_in, cotangent=cotangent, mixer_gain=mixer_gain, mamba_in=mamba_in, state_in=state_in, step_in=step_in, mamba_conv=mamba_conv, state_conv=state_conv, step_bias=step_bias, decay_log=decay_log, skip_gain=skip_gain, query_in=query_in, keyval_in=keyval_in, mamba_out=mamba_out, attention_out=attention_out, feed_gain=feed_gain, gate_up=gate_up, down_weight=down_weight)


rope_base = 100000000000.0
norm_eps = 1e-05

@jax.custom_vjp
def low(v):
    return lax.optimization_barrier(v.astype(jnp.bfloat16)).astype(jnp.float32)

@jax.custom_vjp
def low_back(v):
    return v

def low_keep(v):
    return (low(v), None)

def low_pass(kept, grad):
    return (grad,)

def back_keep(v):
    return (v, None)

def back_low(kept, grad):
    return (low(grad),)
low.defvjp(low_keep, low_pass)
low_back.defvjp(back_keep, back_low)

def matmul(left, right):
    return jnp.dot(left, right, precision=lax.Precision.HIGHEST, preferred_element_type=jnp.float32)

def rms_norm(values, gain_vector):
    inverse_rms = lax.rsqrt(lax.optimization_barrier(jnp.mean(values * values, axis=-1, keepdims=True)) + norm_eps)
    return values * inverse_rms * gain_vector

def causal_conv(signal, kernel):
    kernel_size = kernel.shape[0]
    length = signal.shape[0]
    padded = jnp.pad(signal, ((kernel_size - 1, 0), (0, 0)))
    running = padded[0:length] * kernel[0]
    for offset in range(1, kernel_size):
        running = running + padded[offset:offset + length] * kernel[offset]
    return running

def rotate(values):
    length = values.shape[0]
    half_size = values.shape[-1] // 2
    exponents = jnp.arange(half_size, dtype=jnp.float32) * (-2.0 / values.shape[-1])
    frequency = jnp.power(rope_base, exponents)
    angles = jnp.arange(length, dtype=jnp.float32)[:, None] * frequency[None, :]
    cosine = jnp.cos(angles)[:, None, :]
    sine_part = jnp.sin(angles)[:, None, :]
    first_half = values[..., :half_size]
    second_half = values[..., half_size:]
    return jnp.concatenate([first_half * cosine - second_half * sine_part, second_half * cosine + first_half * sine_part], axis=-1)

def attention(queries, key_heads, value_heads):
    group_size = queries.shape[1] // key_heads.shape[1]
    keys_all = jnp.repeat(key_heads, group_size, axis=1)
    values_all = jnp.repeat(value_heads, group_size, axis=1)
    length = queries.shape[0]
    scores = jnp.einsum('thd,shd->hts', queries, keys_all, precision=lax.Precision.HIGHEST) * queries.shape[-1] ** (-0.5)
    causal = lax.broadcasted_iota(jnp.int32, (length, length), 0) >= lax.broadcasted_iota(jnp.int32, (length, length), 1)
    scores = jnp.where(causal[None], scores, -1e+30)
    row_max = lax.optimization_barrier(jnp.max(scores, axis=-1, keepdims=True))
    weights = jnp.exp(scores - row_max)
    weights = weights / lax.optimization_barrier(jnp.sum(weights, axis=-1, keepdims=True))
    return jnp.einsum('hts,shd->thd', weights, values_all, precision=lax.Precision.HIGHEST)

def state_mix(inputs, state_inputs, state_reads, step_size, decay_log, skip_gain):
    length = inputs.shape[0]
    log_decay = -step_size * jnp.exp(decay_log)[None, :]
    running = jnp.cumsum(log_decay, axis=0)
    causal = lax.broadcasted_iota(jnp.int32, (length, length), 0) >= lax.broadcasted_iota(jnp.int32, (length, length), 1)
    decay_gap = running[:, None, :] - running[None, :, :]
    decays = jnp.exp(jnp.where(causal[:, :, None], decay_gap, -jnp.inf))
    intersection = jnp.dot(state_reads, state_inputs.T, precision=lax.Precision.HIGHEST, preferred_element_type=jnp.float32)
    mixing = intersection[:, :, None] * decays * step_size[None, :, :]
    mixed = jnp.einsum('tsh,shp->thp', mixing, inputs, precision=lax.Precision.HIGHEST)
    return mixed + skip_gain[None, :, None] * inputs

def mixer_core(mamba_proj, state_proj, step_proj, query_proj, keyval_proj, mamba_conv, state_conv, step_bias, decay_log, skip_gain):
    length = mamba_proj.shape[0]
    head_count = step_proj.shape[1]
    gate_part = mamba_proj[:, 0]
    conv_input = jax.nn.silu(causal_conv(mamba_proj[:, 1], mamba_conv))
    conv_state = jax.nn.silu(causal_conv(state_proj, state_conv))
    state_size = state_proj.shape[1] // 2
    step_size = jax.nn.softplus(step_proj + step_bias)
    mixed = state_mix(conv_input.reshape(length, head_count, -1), conv_state[:, :state_size], conv_state[:, state_size:], step_size, decay_log, skip_gain)
    gated_out = mixed.reshape(length, -1) * jax.nn.silu(gate_part)
    queries = rotate(query_proj.reshape(length, -1, HEAD_DIM))
    key_heads = rotate(keyval_proj[:, 0].reshape(length, -1, HEAD_DIM))
    value_heads = keyval_proj[:, 1].reshape(length, -1, HEAD_DIM)
    attended = jax.checkpoint(attention)(queries, key_heads, value_heads).reshape(length, -1)
    return (gated_out, attended)

def swiglu(gate_values):
    return jax.nn.silu(gate_values[:, 0]) * gate_values[:, 1]

def hybrid_layer(weights, hidden):
    mixer_gain, mamba_in, state_in, step_in, mamba_conv, state_conv, step_bias, decay_log, skip_gain, query_in, keyval_in, mamba_out, attention_out, feed_gain, gate_up, down_weight = weights
    length = hidden.shape[0]
    model_width = hidden.shape[1]
    normed = low(rms_norm(hidden, mixer_gain))
    mamba_proj = low_back(matmul(normed, mamba_in.reshape(model_width, -1))).reshape(length, 2, -1)
    state_proj = low_back(matmul(normed, state_in))
    step_proj = low_back(matmul(normed, step_in))
    query_proj = low_back(matmul(normed, query_in))
    keyval_proj = low_back(matmul(normed, keyval_in.reshape(model_width, -1))).reshape(length, 2, -1)
    gated_out, attended = mixer_core(mamba_proj, state_proj, step_proj, query_proj, keyval_proj, mamba_conv, state_conv, step_bias, decay_log, skip_gain)
    branch = low_back(matmul(low(gated_out), mamba_out) + matmul(low(attended), attention_out))
    middle = hidden + branch
    normed_two = low(rms_norm(middle, feed_gain))
    gate_values = low_back(matmul(normed_two, gate_up.reshape(model_width, -1))).reshape(length, 2, -1)
    activated = low(swiglu(gate_values))
    return middle + low_back(matmul(activated, down_weight))

def reference(stream_in, cotangent, mixer_gain, mamba_in, state_in, step_in, mamba_conv, state_conv, step_bias, decay_log, skip_gain, query_in, keyval_in, mamba_out, attention_out, feed_gain, gate_up, down_weight):
    params = tuple((array_item.astype(jnp.float32) for array_item in (mixer_gain, mamba_in, state_in, step_in, mamba_conv, state_conv, step_bias, decay_log, skip_gain, query_in, keyval_in, mamba_out, attention_out, feed_gain, gate_up, down_weight)))
    start = stream_in.astype(jnp.float32)
    seed_grad = cotangent.astype(jnp.float32)

    def run_section(section_params, batch):

        def one_sequence(sequence):
            return hybrid_layer(section_params, sequence)
        return lax.map(jax.checkpoint(one_sequence), batch)
    first_params = tuple((array_item[0] for array_item in params))
    second_params = tuple((array_item[1] for array_item in params))
    middle, first_back = jax.vjp(run_section, first_params, start)
    final, second_back = jax.vjp(run_section, second_params, middle)
    second_grads, middle_grad = second_back(seed_grad)
    first_grads, start_grad = first_back(middle_grad)
    stacked = tuple((jnp.stack([left_item, right_item]) for left_item, right_item in zip(first_grads, second_grads)))
    return (jnp.stack([middle, final]), jnp.stack([start_grad, middle_grad]), stacked[0], stacked[1], stacked[2], stacked[3], stacked[4], stacked[5], stacked[6], stacked[7], stacked[8], stacked[9], stacked[10], stacked[11], stacked[12], stacked[13], stacked[14], stacked[15])
```

```python
import jax
import jax.numpy as jnp
from jax import lax
from jax.experimental import pallas as pl
from jax.experimental.pallas import tpu as pltpu
from jax.sharding import PartitionSpec as P

ATT_HEADS = 8
KV_HEADS = 2
HEAD_DIM = 64
ROWS_IN = 464
ROWS_MIX = 720
ROWS_FEED = 768
ROWS_OWN = ROWS_MIX + ROWS_FEED
ROWS_SHARED = 128
ROWS_ALL = ROWS_OWN + ROWS_SHARED

MESH = pl.DeviceIdType.MESH
DMA = pltpu.SemaphoreType.DMA
bf16 = jnp.bfloat16
f32 = jnp.float32
VMEM = pltpu.VMEM

rope_base = 100000000000.0
norm_eps = 1e-05


def place():
    section = lax.axis_index("section")
    dp = lax.axis_index("dp")
    y = lax.axis_index("tensor")
    return section, dp // 8, (dp // 2) % 4, dp % 2, y


def at_y(y):
    return {"tensor": y}


def at_z(x_hi, z, core):
    return {"dp": x_hi * 8 + z * 2 + core}


def greet(partners):
    barrier = pltpu.get_barrier_semaphore()
    for partner in partners:
        pl.semaphore_signal(barrier, inc=1, device_id=partner, device_id_type=MESH)
    pl.semaphore_wait(barrier, len(partners))


def remote(src, dst, send_sem, recv_sem, partner):
    return pltpu.make_async_remote_copy(
        src_ref=src,
        dst_ref=dst,
        send_sem=send_sem,
        recv_sem=recv_sem,
        device_id=partner,
        device_id_type=MESH,
    )


def kernel_call(body, name, collective, out_shape, args, scratch, in_spaces=None, out_spaces=None):
    in_spaces = in_spaces or [VMEM] * len(args)
    outs = out_shape if isinstance(out_shape, (list, tuple)) else [out_shape]
    out_spaces = out_spaces or [VMEM] * len(outs)
    out_specs = [pl.BlockSpec(memory_space=space) for space in out_spaces]
    return pl.pallas_call(
        body,
        name=name,
        out_shape=out_shape,
        in_specs=[pl.BlockSpec(memory_space=space) for space in in_spaces],
        out_specs=out_specs if isinstance(out_shape, (list, tuple)) else out_specs[0],
        scratch_shapes=scratch,
        compiler_params=pltpu.CompilerParams(
            collective_id=collective, has_side_effects=True, vmem_limit_bytes=56 * 2**20
        ),
    )(*args)


def shape(dims, kind):
    return jax.ShapeDtypeStruct(dims, kind)


def to_chips_body(x_ref, out_ref, send_sem, recv_sem, local_sem):
    _, x_hi, z, core, y = place()
    mine = y // 2
    bit = y % 2
    own = mine == core
    barrier = pltpu.get_barrier_semaphore()
    for b in (0, 1):
        source = {"tensor": 2 * core + b, "dp": x_hi * 8 + z * 2 + mine}
        is_self = jnp.logical_and(own, bit == b)

        @pl.when(jnp.logical_not(is_self))
        def _():
            pl.semaphore_signal(barrier, inc=1, device_id=source, device_id_type=MESH)

    @pl.when(own)
    def _():
        pl.semaphore_wait(barrier, 1)

    @pl.when(jnp.logical_not(own))
    def _():
        pl.semaphore_wait(barrier, 2)

    rows = x_ref.shape[1]
    for j in (0, 1):
        target = {"tensor": 2 * core + j, "dp": x_hi * 8 + z * 2 + mine}
        is_self = jnp.logical_and(own, bit == j)
        slot = out_ref.at[pl.ds(pl.multiple_of(bit * rows, rows), rows)]

        @pl.when(is_self)
        def _():
            pltpu.make_async_copy(x_ref.at[j], slot, local_sem.at[0]).start()

        @pl.when(jnp.logical_not(is_self))
        def _():
            remote(x_ref.at[j], slot, send_sem.at[j], recv_sem.at[bit], target).start()

    for j in (0, 1):
        is_self = jnp.logical_and(own, bit == j)
        slot = out_ref.at[pl.ds(j * rows, rows)]
        target = {"tensor": 2 * core + j, "dp": x_hi * 8 + z * 2 + mine}

        @pl.when(is_self)
        def _():
            pltpu.make_async_copy(x_ref.at[j], slot, local_sem.at[0]).wait()

        @pl.when(jnp.logical_not(is_self))
        def _():
            copy = remote(x_ref.at[j], slot, send_sem.at[j], recv_sem.at[j], target)
            copy.wait_send()
            copy.wait_recv()


def to_chips(x):
    return kernel_call(
        to_chips_body,
        "to_chips",
        1,
        shape((2 * x.shape[1], x.shape[2]), x.dtype),
        (x,),
        [DMA((2,)), DMA((2,)), DMA((1,))],
    )


def from_chips_body(x_ref, out_ref, send_sem, recv_sem, local_sem):
    _, x_hi, z, core, y = place()
    mine = y // 2
    bit = y % 2
    own = mine == core
    barrier = pltpu.get_barrier_semaphore()
    for b in (0, 1):
        source = {"tensor": 2 * core + b, "dp": x_hi * 8 + z * 2 + mine}
        is_self = jnp.logical_and(own, bit == b)

        @pl.when(jnp.logical_not(is_self))
        def _():
            pl.semaphore_signal(barrier, inc=1, device_id=source, device_id_type=MESH)

    @pl.when(own)
    def _():
        pl.semaphore_wait(barrier, 1)

    @pl.when(jnp.logical_not(own))
    def _():
        pl.semaphore_wait(barrier, 2)

    rows = x_ref.shape[0] // 2
    for b in (0, 1):
        target = {"tensor": 2 * core + b, "dp": x_hi * 8 + z * 2 + mine}
        is_self = jnp.logical_and(own, bit == b)
        block = x_ref.at[pl.ds(b * rows, rows)]

        @pl.when(is_self)
        def _():
            pltpu.make_async_copy(block, out_ref.at[bit], local_sem.at[0]).start()

        @pl.when(jnp.logical_not(is_self))
        def _():
            remote(block, out_ref.at[bit], send_sem.at[b], recv_sem.at[bit], target).start()

    for b in (0, 1):
        target = {"tensor": 2 * core + b, "dp": x_hi * 8 + z * 2 + mine}
        is_self = jnp.logical_and(own, bit == b)
        block = x_ref.at[pl.ds(b * rows, rows)]

        @pl.when(is_self)
        def _():
            pltpu.make_async_copy(block, out_ref.at[b], local_sem.at[0]).wait()

        @pl.when(jnp.logical_not(is_self))
        def _():
            copy = remote(block, out_ref.at[b], send_sem.at[b], recv_sem.at[b], target)
            copy.wait_send()
            copy.wait_recv()


def from_chips(x, collective):
    return kernel_call(
        from_chips_body,
        "from_chips",
        collective,
        shape((2, x.shape[0] // 2, x.shape[1]), x.dtype),
        (x,),
        [DMA((2,)), DMA((2,)), DMA((1,))],
    )


def gather_body(mix_ref, feed_ref, small_ref, mix_out, feed_out, small_out, send, recv, local):
    _, x_hi, z, core, y = place()
    right, left, across = (y + 1) % 4, (y + 3) % 4, (y + 2) % 4
    z_right, z_left = at_z(x_hi, (z + 1) % 4, core), at_z(x_hi, (z + 3) % 4, core)
    greet([at_y(right), at_y(left), at_y(across), z_right, z_left])
    counter = [0]

    def go(src, dst, partner):
        n = counter[0]
        counter[0] += 1
        copy = remote(src, dst, send.at[n], recv.at[n], partner)
        copy.start()
        return copy

    def aligned(start, by):
        return pl.multiple_of(start, by)

    feed_at = aligned(z * 192, 192)
    mix_at = aligned(ROWS_IN + z * 64, 16)

    own = []
    for n, (src, dst) in enumerate(
        ((mix_ref, mix_out.at[y]), (feed_ref, feed_out.at[y]), (small_ref, small_out.at[y]))
    ):
        copy = pltpu.make_async_copy(src, dst, local.at[n])
        copy.start()
        own.append(copy)

    helped = (
        (feed_ref, feed_out, feed_at, 0, 192, 96),
        (mix_ref, mix_out, mix_at, 0, 64, 32),
    )
    straight = ((mix_ref, mix_out, 0, 0, ROWS_IN, 240),)
    small = [
        go(small_ref, small_out.at[y], at_y(other)) for other in (right, left, across)
    ]

    def first(group):
        sent = []
        for src, out, start, _, rows, _ in group:
            piece = src.at[pl.ds(start, rows)]
            dst = out.at[y, pl.ds(start, rows)]
            sent.append((go(piece, dst, at_y(right)), go(piece, dst, at_y(left))))
        return sent

    def second(group, sent):
        more = []
        for (src, out, start, _, rows, cut), (to_right, to_left) in zip(group, sent):
            to_right.wait_recv()
            piece = out.at[left, pl.ds(start, cut)]
            a = go(piece, piece, at_y(right))
            to_left.wait_recv()
            piece = out.at[right, pl.ds(start + cut, rows - cut)]
            b = go(piece, piece, at_y(left))
            more.append((a, b))
        return more

    waits = []
    helped_one = first(helped)
    straight_one = first(straight)
    helped_two = second(helped, helped_one)

    def z_first(source_y):
        sent = []
        for src, out, start, _, rows, cut in helped:
            piece = out.at[source_y, pl.ds(start, rows)]
            sent.append((go(piece, piece, z_right), go(piece, piece, z_left)))
        return sent

    def z_second(source_y, sent):
        more = []
        for (src, out, start, _, rows, cut), (to_right, to_left) in zip(helped, sent):
            step = rows
            base = start - z * rows
            from_left = base + ((z + 3) % 4) * rows
            from_right = base + ((z + 1) % 4) * rows
            to_right.wait_recv()
            piece = out.at[source_y, pl.ds(aligned(from_left, 16), cut)]
            a = go(piece, piece, z_right)
            to_left.wait_recv()
            piece = out.at[source_y, pl.ds(aligned(from_right + cut, 16), rows - cut)]
            b = go(piece, piece, z_left)
            more.append((a, b))
        return more

    z_one_left = z_first(left)
    z_one_right = z_first(right)
    straight_two = second(straight, straight_one)
    z_two_left = z_second(left, z_one_left)
    z_two_right = z_second(right, z_one_right)
    for a, b in helped_two:
        a.wait_recv()
        b.wait_recv()
    z_one_across = z_first(across)
    z_two_across = z_second(across, z_one_across)
    for a, b in straight_two:
        a.wait_recv()
        b.wait_recv()
    for group in (z_two_left, z_two_right, z_two_across):
        for a, b in group:
            a.wait_recv()
            b.wait_recv()
    for group in (
        helped_one,
        straight_one,
        helped_two,
        straight_two,
        z_one_left,
        z_one_right,
        z_one_across,
        z_two_left,
        z_two_right,
        z_two_across,
    ):
        for a, b in group:
            a.wait_send()
            b.wait_send()
    for copy in small:
        copy.wait()
    for copy in own:
        copy.wait()


def gather_weights(mix, feed, small):
    any_space = pl.ANY
    return kernel_call(
        gather_body,
        "gather_weights",
        2,
        [
            shape((4,) + mix.shape, mix.dtype),
            shape((4,) + feed.shape, feed.dtype),
            shape((4,) + small.shape, small.dtype),
        ],
        (mix, feed, small),
        [DMA((40,)), DMA((40,)), DMA((3,))],
        [any_space] * 3,
        [any_space] * 3,
    )


def other_core(x_hi, z, core):
    return at_z(x_hi, z, 1 - core)


def inverse_rms(values):
    return lax.rsqrt(jnp.mean(values * values, axis=-1, keepdims=True) + norm_eps)


def my_rows(core, rows):
    return pl.ds(pl.multiple_of(core * rows, rows), rows)


def norm_gather_body(hidden_ref, gain_ref, out_ref, send, recv):
    _, x_hi, z, core, _ = place()
    rows = hidden_ref.shape[0]
    partner = other_core(x_hi, z, core)
    greet([partner])
    hidden = hidden_ref[...]
    out_ref[my_rows(core, rows)] = (hidden * inverse_rms(hidden) * gain_ref[...]).astype(bf16)
    mine = out_ref.at[my_rows(core, rows)]
    copy = remote(mine, mine, send.at[0], recv.at[0], partner)
    copy.start()
    copy.wait()


def norm_gather(hidden, gain, collective):
    return kernel_call(
        norm_gather_body,
        "norm_gather",
        collective,
        shape((2 * hidden.shape[0], hidden.shape[1]), bf16),
        (hidden, gain),
        [DMA((1,)), DMA((1,))],
    )


def cast_gather_body(grad_ref, out_ref, send, recv):
    _, x_hi, z, core, _ = place()
    rows = grad_ref.shape[0]
    partner = other_core(x_hi, z, core)
    greet([partner])
    out_ref[my_rows(core, rows)] = grad_ref[...].astype(bf16)
    mine = out_ref.at[my_rows(core, rows)]
    copy = remote(mine, mine, send.at[0], recv.at[0], partner)
    copy.start()
    copy.wait()


def cast_gather(grad, collective):
    return kernel_call(
        cast_gather_body,
        "cast_gather",
        collective,
        shape((2 * grad.shape[0], grad.shape[1]), bf16),
        (grad,),
        [DMA((1,)), DMA((1,))],
    )


def swap_halves(part_ref, land, send, recv, partner, core):
    rows = land.shape[0]
    copy = remote(part_ref.at[my_rows(1 - core, rows)], land, send, recv, partner)
    copy.start()
    copy.wait()
    return part_ref[my_rows(core, rows)].astype(f32) + land[...].astype(f32)


def middle_body(part_ref, hidden_ref, gain_ref, middle_ref, out_ref, land, send, recv):
    _, x_hi, z, core, _ = place()
    rows = hidden_ref.shape[0]
    partner = other_core(x_hi, z, core)
    greet([partner])
    branch = swap_halves(part_ref, land, send.at[0], recv.at[0], partner, core)
    middle = hidden_ref[...] + branch
    middle_ref[...] = middle
    out_ref[my_rows(core, rows)] = (middle * inverse_rms(middle) * gain_ref[...]).astype(bf16)
    mine = out_ref.at[my_rows(core, rows)]
    copy = remote(mine, mine, send.at[1], recv.at[1], partner)
    copy.start()
    copy.wait()


def middle_step(part, hidden, gain, collective):
    rows, width = hidden.shape
    return kernel_call(
        middle_body,
        "middle_step",
        collective,
        [shape((rows, width), f32), shape((2 * rows, width), bf16)],
        (part, hidden, gain),
        [VMEM((rows, width), bf16), DMA((2,)), DMA((2,))],
    )


def output_body(part_ref, middle_ref, out_ref, received_ref, land, low, send, recv):
    section, x_hi, z, core, _ = place()
    partner = other_core(x_hi, z, core)
    beyond = {"section": 1 - section}
    greet([partner, beyond])
    out = middle_ref[...] + swap_halves(part_ref, land, send.at[0], recv.at[0], partner, core)
    out_ref[...] = out
    low[...] = out.astype(bf16)
    copy = remote(low, received_ref, send.at[1], recv.at[1], beyond)
    copy.start()
    copy.wait()


def output_step(part, middle, collective):
    rows, width = middle.shape
    return kernel_call(
        output_body,
        "output_step",
        collective,
        [shape((rows, width), f32), shape((rows, width), bf16)],
        (part, middle),
        [VMEM((rows, width), bf16), VMEM((rows, width), bf16), DMA((2,)), DMA((2,))],
    )


def rms_back(values, gain, grad):
    scale = inverse_rms(values)
    weighted = grad * gain
    unit = values * scale
    inner = jnp.mean(weighted * unit, axis=-1, keepdims=True)
    return scale * (weighted - unit * inner), jnp.sum(grad * unit, axis=0, keepdims=True)


def middle_back_body(
    part_ref, middle_ref, gain_ref, grad_ref, out_ref, full_ref, gain_grad_ref, land, send, recv
):
    _, x_hi, z, core, _ = place()
    rows = middle_ref.shape[0]
    partner = other_core(x_hi, z, core)
    greet([partner])
    normed_grad = swap_halves(part_ref, land, send.at[0], recv.at[0], partner, core)
    back, gain_grad = rms_back(middle_ref[...], gain_ref[...], normed_grad)
    gain_grad_ref[...] = gain_grad
    grad = grad_ref[...] + back
    out_ref[...] = grad
    full_ref[my_rows(core, rows)] = grad.astype(bf16)
    mine = full_ref.at[my_rows(core, rows)]
    copy = remote(mine, mine, send.at[1], recv.at[1], partner)
    copy.start()
    copy.wait()


def middle_back(part, middle, gain, grad, collective):
    rows, width = middle.shape
    return kernel_call(
        middle_back_body,
        "middle_back",
        collective,
        [shape((rows, width), f32), shape((2 * rows, width), bf16), shape((1, width), f32)],
        (part, middle, gain, grad),
        [VMEM((rows, width), bf16), DMA((2,)), DMA((2,))],
    )


def input_back_body(
    part_ref, hidden_ref, gain_ref, grad_ref, out_ref, received_ref, gain_grad_ref, land, low, send, recv
):
    section, x_hi, z, core, _ = place()
    partner = other_core(x_hi, z, core)
    beyond = {"section": 1 - section}
    greet([partner, beyond])
    normed_grad = swap_halves(part_ref, land, send.at[0], recv.at[0], partner, core)
    back, gain_grad = rms_back(hidden_ref[...], gain_ref[...], normed_grad)
    gain_grad_ref[...] = gain_grad
    grad = grad_ref[...] + back
    out_ref[...] = grad
    low[...] = grad.astype(bf16)
    copy = remote(low, received_ref, send.at[1], recv.at[1], beyond)
    copy.start()
    copy.wait()


def input_back(part, hidden, gain, grad, collective):
    rows, width = hidden.shape
    return kernel_call(
        input_back_body,
        "input_back",
        collective,
        [shape((rows, width), f32), shape((rows, width), bf16), shape((1, width), f32)],
        (part, hidden, gain, grad),
        [VMEM((rows, width), bf16), VMEM((rows, width), bf16), DMA((2,)), DMA((2,))],
    )


CUT_ONE = 816
CUT_HALF = 416


def add_into(dst, sources, rows, strip):
    def step(n, carry):
        at = pl.ds(pl.multiple_of(n * strip, 16), strip)
        total = sources[0][at].astype(f32)
        for source in sources[1:]:
            total = total + source[at].astype(f32)
        dst[at] = total.astype(dst.dtype)
        return carry

    lax.fori_loop(0, rows // strip, step, 0)


def reduce_body(
    grads,
    small_ref,
    out_ref,
    shared_ref,
    small_out,
    land_y,
    land_z,
    sum_y,
    sum_z,
    land_yz,
    land_zy,
    both,
    land_x,
    small_y,
    small_z,
    small_x,
    small_sum,
    send,
    recv,
):
    _, x_hi, z, core, y = place()
    right, left, across = (y + 1) % 4, (y + 3) % 4, (y + 2) % 4
    y_right, y_left, y_across = at_y(right), at_y(left), at_y(across)
    z_r, z_l, z_a = (z + 1) % 4, (z + 3) % 4, (z + 2) % 4
    z_right, z_left, z_across = (at_z(x_hi, k, core) for k in (z_r, z_l, z_a))
    x_other = at_z(1 - x_hi, z, core)
    partner = other_core(x_hi, z, core)
    greet([y_right, y_left, y_across, z_right, z_left, z_across, x_other, partner])
    counter = [0]
    started = []

    def go(src, dst, to):
        n = counter[0]
        counter[0] += 1
        copy = remote(src, dst, send.at[n], recv.at[n], to)
        copy.start()
        started.append(copy)
        return copy

    top = (0, CUT_HALF)
    low = (CUT_HALF, CUT_ONE - CUT_HALF)
    rest = ROWS_ALL - CUT_ONE
    rest_half = rest // 2

    def lanes(k):
        return pl.ds(pl.multiple_of(k * 256, 256), 256)

    def one(k, piece):
        return grads.at[k, pl.ds(*piece)]

    a1 = go(one(across, top), land_y.at[0, pl.ds(*top)], y_right)
    b1 = go(one(across, low), land_y.at[0, pl.ds(*low)], y_left)

    def two(k, pair):
        return grads.at[pl.ds(pair, 2), pl.ds(CUT_ONE, rest), lanes(k)]

    a2 = go(two(z_a, 0), land_z.at[0, pl.ds(0, 2)], z_right)
    b2 = go(two(z_a, 2), land_z.at[0, pl.ds(2, 2)], z_left)
    e1 = go(one(right, low), land_y.at[1, pl.ds(*low)], y_right)
    f1 = go(one(left, top), land_y.at[2, pl.ds(*top)], y_left)
    e2 = go(two(z_r, 2), land_z.at[1, pl.ds(2, 2)], z_right)
    f2 = go(two(z_l, 0), land_z.at[2, pl.ds(0, 2)], z_left)

    s_y = [go(small_ref, small_y.at[n], to) for n, to in enumerate((y_right, y_left, y_across))]
    for copy in s_y:
        copy.wait_recv()
    small_sum[0] = small_ref[...] + small_y[0] + small_y[1] + small_y[2]
    s_z = [go(small_sum.at[0], small_z.at[n], to) for n, to in enumerate((z_right, z_left, z_across))]

    a1.wait_recv()
    add_into(land_y.at[0, pl.ds(*top)], (one(right, top), land_y.at[0, pl.ds(*top)]), top[1], 32)
    c1 = go(land_y.at[0, pl.ds(*top)], land_y.at[1, pl.ds(*top)], y_right)
    b1.wait_recv()
    add_into(land_y.at[0, pl.ds(*low)], (one(left, low), land_y.at[0, pl.ds(*low)]), low[1], 80)
    d1 = go(land_y.at[0, pl.ds(*low)], land_y.at[2, pl.ds(*low)], y_left)
    a2.wait_recv()
    for k in (0, 1):
        mine = grads.at[k, pl.ds(CUT_ONE, rest), lanes(z_r)]
        add_into(land_z.at[0, k], (mine, land_z.at[0, k]), rest, 80)
    c2 = go(land_z.at[0, pl.ds(0, 2)], land_z.at[1, pl.ds(0, 2)], z_right)
    b2.wait_recv()
    for k in (2, 3):
        mine = grads.at[k, pl.ds(CUT_ONE, rest), lanes(z_l)]
        add_into(land_z.at[0, k], (mine, land_z.at[0, k]), rest, 80)
    d2 = go(land_z.at[0, pl.ds(2, 2)], land_z.at[2, pl.ds(2, 2)], z_left)

    for copy in s_z:
        copy.wait_recv()
    small_sum[1] = small_sum[0] + small_z[0] + small_z[1] + small_z[2]
    s_x = go(small_sum.at[1], small_x.at[0], x_other)

    for copy in (e1, f1, c1, d1):
        copy.wait_recv()
    add_into(sum_y, (grads.at[y, pl.ds(0, CUT_ONE)], land_y.at[1], land_y.at[2]), CUT_ONE, 48)

    def one_z(k, piece):
        return sum_y.at[pl.ds(*piece), lanes(k)]

    a3 = go(one_z(z_a, top), land_yz.at[0, pl.ds(*top)], z_right)
    b3 = go(one_z(z_a, low), land_yz.at[0, pl.ds(*low)], z_left)
    e3 = go(one_z(z_r, low), land_yz.at[1, pl.ds(*low)], z_right)
    f3 = go(one_z(z_l, top), land_yz.at[2, pl.ds(*top)], z_left)

    for copy in (e2, f2, c2, d2):
        copy.wait_recv()
    for k in range(4):
        mine = grads.at[k, pl.ds(CUT_ONE, rest), lanes(z)]
        add_into(sum_z.at[k], (mine, land_z.at[1, k], land_z.at[2, k]), rest, 80)

    def two_y(k, start):
        return sum_z.at[k, pl.ds(start, rest_half)]

    a4 = go(two_y(across, 0), land_zy.at[0, pl.ds(0, rest_half)], y_right)
    b4 = go(two_y(across, rest_half), land_zy.at[0, pl.ds(rest_half, rest_half)], y_left)
    e4 = go(two_y(right, rest_half), land_zy.at[1, pl.ds(rest_half, rest_half)], y_right)
    f4 = go(two_y(left, 0), land_zy.at[2, pl.ds(0, rest_half)], y_left)

    s_x.wait_recv()
    small_sum[2] = small_sum[1] + small_x[0]
    s_c = go(small_sum.at[2], small_out.at[core], partner)
    small_out[core] = small_sum[2]

    a3.wait_recv()
    add_into(land_yz.at[0, pl.ds(*top)], (one_z(z_r, top), land_yz.at[0, pl.ds(*top)]), top[1], 32)
    c3 = go(land_yz.at[0, pl.ds(*top)], land_yz.at[1, pl.ds(*top)], z_right)
    b3.wait_recv()
    add_into(land_yz.at[0, pl.ds(*low)], (one_z(z_l, low), land_yz.at[0, pl.ds(*low)]), low[1], 80)
    d3 = go(land_yz.at[0, pl.ds(*low)], land_yz.at[2, pl.ds(*low)], z_left)
    a4.wait_recv()
    first = pl.ds(0, rest_half)
    second = pl.ds(rest_half, rest_half)
    add_into(land_zy.at[0, first], (two_y(right, 0), land_zy.at[0, first]), rest_half, 80)
    c4 = go(land_zy.at[0, first], land_zy.at[1, first], y_right)
    b4.wait_recv()
    add_into(land_zy.at[0, second], (two_y(left, rest_half), land_zy.at[0, second]), rest_half, 80)
    d4 = go(land_zy.at[0, second], land_zy.at[2, second], y_left)

    for copy in (e3, f3, c3, d3):
        copy.wait_recv()
    add_into(
        both.at[pl.ds(0, CUT_ONE)],
        (sum_y.at[:, lanes(z)], land_yz.at[1], land_yz.at[2]),
        CUT_ONE,
        48,
    )

    def half(k):
        return pl.ds(pl.multiple_of(k * 128, 128), 128)

    part_one = pl.ds(0, CUT_ONE)
    part_two = pl.ds(CUT_ONE, rest)
    x1 = go(both.at[part_one, half(1 - x_hi)], land_x.at[part_one], x_other)
    for copy in (e4, f4, c4, d4):
        copy.wait_recv()
    add_into(both.at[part_two], (sum_z.at[y], land_zy.at[1], land_zy.at[2]), rest, 80)
    x2 = go(both.at[part_two, half(1 - x_hi)], land_x.at[part_two], x_other)
    x1.wait_recv()
    add_into(
        out_ref.at[core, part_one], (both.at[part_one, half(x_hi)], land_x.at[part_one]), CUT_ONE, 48
    )
    k1 = go(out_ref.at[core, part_one], out_ref.at[core, part_one], partner)
    x2.wait_recv()
    add_into(
        out_ref.at[core, part_two], (both.at[part_two, half(x_hi)], land_x.at[part_two]), rest, 80
    )
    k2 = go(out_ref.at[core, part_two], out_ref.at[core, part_two], partner)
    k1.wait_recv()
    k2.wait_recv()
    shared_at = pl.ds(ROWS_OWN, ROWS_SHARED)
    shared_ref[y] = out_ref[0, shared_at] + out_ref[1, shared_at]
    ends = [go(shared_ref.at[y], shared_ref.at[y], to) for to in (y_right, y_left, y_across)]
    s_c.wait_recv()
    for copy in ends:
        copy.wait_recv()
    for copy in started:
        copy.wait_send()


def reduce_grads(grads, small, collective):
    rest = ROWS_ALL - CUT_ONE
    return kernel_call(
        reduce_body,
        "reduce_grads",
        collective,
        [
            shape((2, ROWS_ALL, 128), f32),
            shape((4, ROWS_SHARED, 128), f32),
            shape((2,) + small.shape, f32),
        ],
        (grads, small),
        [
            VMEM((3, CUT_ONE, 1024), bf16),
            VMEM((3, 4, rest, 256), bf16),
            VMEM((CUT_ONE, 1024), bf16),
            VMEM((4, rest, 256), bf16),
            VMEM((3, CUT_ONE, 256), bf16),
            VMEM((3, rest, 256), bf16),
            VMEM((ROWS_ALL, 256), bf16),
            VMEM((ROWS_ALL, 128), bf16),
            VMEM((3,) + small.shape, f32),
            VMEM((3,) + small.shape, f32),
            VMEM((1,) + small.shape, f32),
            VMEM((3,) + small.shape, f32),
            DMA((40,)),
            DMA((40,)),
        ],
    )


def causal_conv(signal, kernel):
    kernel_size = kernel.shape[0]
    length = signal.shape[0]
    padded = jnp.pad(signal, ((kernel_size - 1, 0), (0, 0)))
    running = padded[0:length] * kernel[0]
    for offset in range(1, kernel_size):
        running = running + padded[offset : offset + length] * kernel[offset]
    return running


def rotate(values):
    length = values.shape[0]
    half_size = values.shape[-1] // 2
    exponents = jnp.arange(half_size, dtype=jnp.float32) * (-2.0 / values.shape[-1])
    frequency = jnp.power(rope_base, exponents)
    angles = jnp.arange(length, dtype=jnp.float32)[:, None] * frequency[None, :]
    cosine = jnp.cos(angles)[:, None, :]
    sine_part = jnp.sin(angles)[:, None, :]
    first_half = values[..., :half_size]
    second_half = values[..., half_size:]
    return jnp.concatenate(
        [
            first_half * cosine - second_half * sine_part,
            second_half * cosine + first_half * sine_part,
        ],
        axis=-1,
    )


def attention(queries, key_heads, value_heads):
    group_size = queries.shape[1] // key_heads.shape[1]
    keys_all = jnp.repeat(key_heads, group_size, axis=1)
    values_all = jnp.repeat(value_heads, group_size, axis=1)
    length = queries.shape[0]
    scores = jnp.einsum(
        "thd,shd->hts", queries, keys_all
    ) * queries.shape[-1] ** (-0.5)
    causal = lax.broadcasted_iota(jnp.int32, (length, length), 0) >= lax.broadcasted_iota(
        jnp.int32, (length, length), 1
    )
    scores = jnp.where(causal[None], scores, -1e30)
    row_max = jnp.max(scores, axis=-1, keepdims=True)
    weights = jnp.exp(scores - row_max)
    weights = weights / jnp.sum(weights, axis=-1, keepdims=True)
    return jnp.einsum("hts,shd->thd", weights, values_all)


def state_mix(inputs, state_inputs, state_reads, step_size, decay_log, skip_gain):
    length = inputs.shape[0]
    log_decay = -step_size * jnp.exp(decay_log)[None, :]
    running = jnp.cumsum(log_decay, axis=0)
    causal = lax.broadcasted_iota(jnp.int32, (length, length), 0) >= lax.broadcasted_iota(
        jnp.int32, (length, length), 1
    )
    decay_gap = running[:, None, :] - running[None, :, :]
    decays = jnp.exp(jnp.where(causal[:, :, None], decay_gap, -jnp.inf))
    intersection = jnp.dot(state_reads, state_inputs.T, preferred_element_type=jnp.float32)
    mixing = intersection[:, :, None] * decays * step_size[None, :, :]
    mixed = jnp.einsum("tsh,shp->thp", mixing, inputs)
    return mixed + skip_gain[None, :, None] * inputs


def mixer_core(
    mamba_proj,
    state_proj,
    step_proj,
    query_proj,
    keyval_proj,
    mamba_conv,
    state_conv,
    step_bias,
    decay_log,
    skip_gain,
):
    length = mamba_proj.shape[0]
    head_count = step_proj.shape[1]
    gate_part = mamba_proj[:, 0]
    conv_input = jax.nn.silu(causal_conv(mamba_proj[:, 1], mamba_conv))
    conv_state = jax.nn.silu(causal_conv(state_proj, state_conv))
    state_size = state_proj.shape[1] // 2
    step_size = jax.nn.softplus(step_proj + step_bias)
    mixed = state_mix(
        conv_input.reshape(length, head_count, -1),
        conv_state[:, :state_size],
        conv_state[:, state_size:],
        step_size,
        decay_log,
        skip_gain,
    )
    gated_out = mixed.reshape(length, -1) * jax.nn.silu(gate_part)
    queries = rotate(query_proj.reshape(length, -1, HEAD_DIM))
    key_heads = rotate(keyval_proj[:, 0].reshape(length, -1, HEAD_DIM))
    value_heads = keyval_proj[:, 1].reshape(length, -1, HEAD_DIM)
    attended = jax.checkpoint(attention)(queries, key_heads, value_heads).reshape(length, -1)
    return (gated_out, attended)


def swiglu(gate, up):
    return jax.nn.silu(gate) * up


def product(left, right):
    return jnp.dot(left, right, preferred_element_type=jnp.float32)


def product_t(left, right):
    return lax.dot_general(left, right, (((1,), (1,)), ((), ())), preferred_element_type=jnp.float32)


def outer_sum(left, right):
    return lax.dot_general(left, right, (((0,), (0,)), ((), ())), preferred_element_type=jnp.float32)


def rows_of(pack, start, stop):
    part = pack[:, start:stop]
    return part.reshape(-1, part.shape[-1])


def per_device(
    stream_in,
    cotangent,
    mixer_gain,
    mamba_in,
    state_in,
    step_in,
    mamba_conv,
    state_conv,
    step_bias,
    decay_log,
    skip_gain,
    query_in,
    keyval_in,
    mamba_out,
    attention_out,
    feed_gain,
    gate_up,
    down_weight,
):
    section, x_hi, z, core, y = place()
    is_first = section == 0
    width = stream_in.shape[2]
    length = 4 * stream_in.shape[1]
    gain_one = mixer_gain.astype(f32)
    gain_two = feed_gain.astype(f32)

    def mine(values, axis):
        size = values.shape[axis] // 2
        return lax.dynamic_slice_in_dim(values, core * size, size, axis)

    def turned(values):
        return mine(values, 1).T

    step_rows = jnp.pad(turned(step_in[0]), ((0, 13), (0, 0)))
    mix = jnp.concatenate(
        [
            turned(mamba_in[0, :, 0]),
            turned(mamba_in[0, :, 1]),
            turned(query_in[0]),
            step_rows,
            mine(mamba_out[0], 0),
            mine(attention_out[0], 0),
        ]
    )
    feed = jnp.concatenate(
        [turned(gate_up[0, :, 0]), turned(gate_up[0, :, 1]), mine(down_weight[0], 0)]
    )
    conv_mine = jnp.pad(mine(mamba_conv[0].astype(f32), 1), ((0, 0), (0, 64)))
    heads_mine = jnp.pad(
        jnp.stack([mine(step_bias[0], 0), mine(decay_log[0], 0), mine(skip_gain[0], 0)]),
        ((0, 9), (0, 253)),
    )
    mix_all, feed_all, small_all = gather_weights(
        mix, feed, jnp.concatenate([conv_mine, heads_mine])
    )
    shared = jnp.concatenate(
        [state_in[0].T, keyval_in[0, :, 0].T, keyval_in[0, :, 1].T]
    )
    conv_x = small_all[:, 0:4, 0:192].transpose(1, 0, 2).reshape(4, 768)
    bias = small_all[:, 4, 0:3].reshape(12)
    decay = small_all[:, 5, 0:3].reshape(12)
    skip = small_all[:, 6, 0:3].reshape(12)
    conv_state_f = state_conv[0].astype(f32)

    w_mamba = jnp.concatenate([rows_of(mix_all, 0, 192), rows_of(mix_all, 192, 384)])
    w_query = rows_of(mix_all, 384, 448)
    w_step = rows_of(mix_all, 448, 451)
    w_mamba_out = rows_of(mix_all, 464, 656)
    w_att_out = rows_of(mix_all, 656, 720)
    w_gate = rows_of(feed_all, 0, 256)
    w_up = rows_of(feed_all, 256, 512)
    w_down = rows_of(feed_all, 512, 768)

    own = to_chips(jnp.where(is_first, stream_in, cotangent)).astype(f32)

    def forward(hidden, ids):
        normed = norm_gather(hidden, gain_one, ids[0])
        mamba_proj = product_t(normed, w_mamba).reshape(length, 2, -1)
        shared_proj = product_t(normed, shared)
        step_proj = product_t(normed, w_step)
        query_proj = product_t(normed, w_query)
        core_values, core_back = jax.vjp(
            mixer_core,
            mamba_proj,
            shared_proj[:, :256],
            step_proj,
            query_proj,
            shared_proj[:, 256:].reshape(length, 2, -1),
            conv_x,
            conv_state_f,
            bias,
            decay,
            skip,
        )
        gated = core_values[0].astype(bf16)
        attended = core_values[1].astype(bf16)
        part = (product(gated, w_mamba_out) + product(attended, w_att_out)).astype(bf16)
        middle, normed_two = middle_step(part, hidden, gain_two, ids[1])
        gate = product_t(normed_two, w_gate)
        up = product_t(normed_two, w_up)
        activated = swiglu(gate, up).astype(bf16)
        part_two = product(activated, w_down).astype(bf16)
        out, received = output_step(part_two, middle, ids[2])
        record = (hidden, normed, core_back, gated, attended, middle, normed_two, gate, up, activated)
        return out, received, record

    def backward(grad_out, record, ids, weights_too):
        hidden, normed, core_back, gated, attended, middle, normed_two, gate, up, activated = record
        feed_grad = cast_gather(grad_out, ids[0])
        activated_grad = product_t(feed_grad, w_down)
        gate_grad, up_grad = jax.vjp(swiglu, gate, up)[1](activated_grad)
        gate_grad = gate_grad.astype(bf16)
        up_grad = up_grad.astype(bf16)
        part = (product(gate_grad, w_gate) + product(up_grad, w_up)).astype(bf16)
        middle_grad, branch_grad, gain_two_grad = middle_back(part, middle, gain_two, grad_out, ids[1])
        core_grads = core_back(
            (product_t(branch_grad, w_mamba_out), product_t(branch_grad, w_att_out))
        )
        mamba_grad = core_grads[0].reshape(length, -1).astype(bf16)
        state_grad = core_grads[1].astype(bf16)
        step_grad = core_grads[2].astype(bf16)
        query_grad = core_grads[3].astype(bf16)
        keyval_grad = core_grads[4].reshape(length, -1).astype(bf16)
        shared_grad = jnp.concatenate([state_grad, keyval_grad], axis=1)
        part_two = (
            product(mamba_grad, w_mamba)
            + product(shared_grad, shared)
            + product(step_grad, w_step)
            + product(query_grad, w_query)
        ).astype(bf16)
        grad_in, received, gain_one_grad = input_back(
            part_two, hidden, gain_one, middle_grad, ids[2]
        )
        if not weights_too:
            return received
        step_slots = jnp.pad(step_grad.reshape(length, 4, 3), ((0, 0), (0, 0), (0, 13)))

        def by_y(values):
            return values.reshape(length, 4, -1)

        left_in = jnp.concatenate(
            [
                by_y(mamba_grad[:, :768]),
                by_y(mamba_grad[:, 768:]),
                by_y(query_grad),
                step_slots,
            ],
            axis=2,
        )
        left_branch = jnp.concatenate([by_y(gated), by_y(attended)], axis=2)
        left_two = jnp.concatenate([by_y(gate_grad), by_y(up_grad)], axis=2)

        def sums(left, right):
            return jnp.einsum("tyr,td->yrd", left, right, preferred_element_type=f32)

        grads = jnp.concatenate(
            [
                sums(left_in, normed),
                sums(left_branch, branch_grad),
                sums(left_two, normed_two),
                sums(by_y(activated), feed_grad),
                sums(by_y(shared_grad), normed),
            ],
            axis=1,
        ).astype(bf16)
        grads = (
            grads.reshape(4, ROWS_ALL, 2, 4, 128).transpose(0, 1, 3, 2, 4).reshape(4, ROWS_ALL, 1024)
        )
        heads = jnp.pad(jnp.concatenate(core_grads[7:10]), (0, 1024 - 36))
        small = jnp.concatenate(
            [
                gain_one_grad,
                gain_two_grad,
                core_grads[6].reshape(1, 1024),
                core_grads[5].reshape(3, 1024),
                heads[None],
                jnp.zeros((1, 1024), f32),
            ]
        )
        return grad_in, grads, small

    _, received, _ = forward(own, (3, 4, 5))
    hidden = jnp.where(is_first, own, received.astype(f32))
    out, _, record = forward(hidden, (6, 7, 8))
    received = backward(own, record, (9, 10, 11), False)
    grad_out = jnp.where(is_first, received.astype(f32), own)
    grad_in, grads, small = backward(grad_out, record, (12, 13, 14), True)
    reduced, shared_sum, small_sum = reduce_grads(grads, small, 15)

    section_output = from_chips(out.astype(bf16), 16).astype(f32)[None]
    input_grad = from_chips(grad_in.astype(bf16), 17).astype(f32)[None]

    lanes = lax.dynamic_slice_in_dim(reduced, core * 64, 64, 2)

    def rows(start, stop):
        return lanes[:, start:stop].reshape(-1, 64)

    def pair(first, second):
        return jnp.stack([rows(*first).T, rows(*second).T], axis=1)[None]

    shared_mine = lax.dynamic_slice_in_dim(shared_sum, core * 64 + y * 16, 16, 2)
    shared_mine = shared_mine.reshape(512, 16).T
    small_both = small_sum[0] + small_sum[1]
    tiny_at = (x_hi * 8 + z * 2 + core) * 4 + y
    gains = lax.dynamic_slice_in_dim(small_both[0:2], tiny_at * 16, 16, 1)
    conv_state_grad = lax.dynamic_slice_in_dim(small_both[2].reshape(4, 256), tiny_at * 4, 4, 1)
    conv_both = lax.dynamic_slice_in_dim(
        small_sum[:, 3:6].reshape(2, 4, 4, 192), y, 1, 2
    )[:, :, 0]
    conv_grad = conv_both.transpose(1, 0, 2).reshape(4, 384)
    heads_both = lax.dynamic_slice_in_dim(
        small_sum[:, 6, :36].reshape(2, 3, 4, 3), y, 1, 2
    )[:, :, 0]
    heads_grad = heads_both.transpose(1, 0, 2).reshape(3, 6)
    return (
        section_output,
        input_grad,
        gains[0][None],
        pair((0, 192), (192, 384)),
        shared_mine[:, :256][None],
        rows(448, 451).T[None],
        conv_grad[None],
        conv_state_grad[None],
        heads_grad[0][None],
        heads_grad[1][None],
        heads_grad[2][None],
        rows(384, 448).T[None],
        shared_mine[:, 256:].reshape(16, 2, 128)[None],
        rows(464, 656)[None],
        rows(656, 720)[None],
        gains[1][None],
        pair((720, 976), (976, 1232)),
        rows(1232, 1488)[None],
    )


def solution(mesh):
    in_specs = (
        P("dp", "tensor", None),
        P("dp", "tensor", None),
        P("section", None),
        P("section", None, None, "tensor"),
        P("section", None, None),
        P("section", None, "tensor"),
        P("section", None, "tensor"),
        P("section", None, None),
        P("section", "tensor"),
        P("section", "tensor"),
        P("section", "tensor"),
        P("section", None, "tensor"),
        P("section", None, None, None),
        P("section", "tensor", None),
        P("section", "tensor", None),
        P("section", None),
        P("section", None, None, "tensor"),
        P("section", "tensor", None),
    )
    out_specs = (
        P("section", "dp", "tensor", None),
        P("section", "dp", "tensor", None),
        P("section", ("dp", "tensor")),
        P("section", "dp", None, "tensor"),
        P("section", ("dp", "tensor"), None),
        P("section", "dp", "tensor"),
        P("section", None, "tensor"),
        P("section", None, ("dp", "tensor")),
        P("section", "tensor"),
        P("section", "tensor"),
        P("section", "tensor"),
        P("section", "dp", "tensor"),
        P("section", ("dp", "tensor"), None, None),
        P("section", "tensor", "dp"),
        P("section", "tensor", "dp"),
        P("section", ("dp", "tensor")),
        P("section", "dp", None, "tensor"),
        P("section", "tensor", "dp"),
    )
    return jax.shard_map(
        per_device, mesh=mesh, in_specs=in_specs, out_specs=out_specs, check_vma=False
    )
```

```python
import functools
import math
import types

import jax
import jax.numpy as jnp
from jax import lax
from jax.experimental import pallas as pl
from jax.experimental.pallas import tpu as pltpu
from jax.sharding import PartitionSpec as P

ROWS_MIX = 720
ROWS_FEED = 768
ROWS_OUT = 704
ROWS_SHARED = 128
ROWS_EXTRA = ROWS_SHARED + 16
ROWS_ALL = ROWS_FEED + ROWS_OUT + ROWS_EXTRA

MESH = pl.DeviceIdType.MESH
DMA = pltpu.SemaphoreType.DMA
bf16 = jnp.bfloat16
f32 = jnp.float32
VMEM = pltpu.VMEM
ANY = pl.ANY
HIGH = lax.Precision.HIGHEST
CHUNK = 128
CHUNKS = 5
LANES = 192
NN = ((1,), (0,))
NT = ((1,), (1,))
TN = ((0,), (0,))

rope_base = 100000000000.0
norm_eps = 1e-05


SECTION, DP, TENSOR = "section", "dp", "tensor"


def place():
    section = lax.axis_index(SECTION)
    dp = lax.axis_index(DP)
    y = lax.axis_index(TENSOR)
    return section, dp // 8, (dp // 2) % 4, dp % 2, y


def at_y(y):
    return {TENSOR: y}


def at_z(x_hi, z, core):
    return {DP: x_hi * 8 + z * 2 + core}


def greet(partners):
    barrier = pltpu.get_barrier_semaphore()
    for partner in partners:
        pl.semaphore_signal(barrier, inc=1, device_id=partner, device_id_type=MESH)
    pl.semaphore_wait(barrier, len(partners))


def remote(src, dst, send_sem, recv_sem, partner):
    return pltpu.make_async_remote_copy(
        src_ref=src,
        dst_ref=dst,
        send_sem=send_sem,
        recv_sem=recv_sem,
        device_id=partner,
        device_id_type=MESH,
    )


class Copies:
    def __init__(self, send, recv):
        self.send, self.recv, self.table, self.gone = send, recv, {}, set()

    def add(self, name, src, dst, partner):
        self.table[name] = (src, dst, len(self.table), partner)

    def of(self, name):
        src, dst, n, partner = self.table[name]
        return remote(src, dst, self.send.at[n], self.recv.at[n], partner)

    def start(self, *names):
        for name in names:
            self.of(name).start()

    def arrive(self, *names):
        for name in names:
            self.of(name).wait_recv()

    def left(self, *names):
        for name in names:
            self.of(name).wait_send()
            self.gone.add(name)

    def leave(self):
        self.left(*(name for name in self.table if name not in self.gone))


def shape(dims, kind):
    return jax.ShapeDtypeStruct(dims, kind)


def kernel_call(body, name, collective, out_shape, args, scratch, in_spaces=None, out_spaces=None):
    in_spaces = in_spaces or [VMEM] * len(args)
    outs = out_shape if isinstance(out_shape, (list, tuple)) else [out_shape]
    out_spaces = out_spaces or [VMEM] * len(outs)
    out_specs = [pl.BlockSpec(memory_space=space) for space in out_spaces]
    return pl.pallas_call(
        body,
        name=name,
        out_shape=out_shape,
        in_specs=[pl.BlockSpec(memory_space=space) for space in in_spaces],
        out_specs=out_specs if isinstance(out_shape, (list, tuple)) else out_specs[0],
        scratch_shapes=scratch,
        compiler_params=pltpu.CompilerParams(
            collective_id=collective, has_side_effects=True, vmem_limit_bytes=56 * 2**20
        ),
    )(*args)


def mm(left, right, dims, precision=None):
    return lax.dot_general(
        left, right, (dims, ((), ())), precision=precision, preferred_element_type=f32
    )


class Swap:
    def __init__(self, send, recv, local):
        _, x_hi, z, core, y = place()
        self.send, self.recv, self.local = send, recv, local
        self.bit = y % 2
        self.own = y // 2 == core
        self.partners = [
            {TENSOR: 2 * core + n, DP: x_hi * 8 + z * 2 + y // 2} for n in (0, 1)
        ]

    def stays(self, n):
        return jnp.logical_and(self.own, self.bit == n)

    def greet(self, others):
        barrier = pltpu.get_barrier_semaphore()
        for partner in others:
            pl.semaphore_signal(barrier, inc=1, device_id=partner, device_id_type=MESH)
        for n in (0, 1):

            @pl.when(jnp.logical_not(self.stays(n)))
            def _():
                pl.semaphore_signal(
                    barrier, inc=1, device_id=self.partners[n], device_id_type=MESH
                )

        @pl.when(self.own)
        def _():
            pl.semaphore_wait(barrier, len(others) + 1)

        @pl.when(jnp.logical_not(self.own))
        def _():
            pl.semaphore_wait(barrier, len(others) + 2)

    def start(self, block, slot, condition=None):
        def also(test):
            return test if condition is None else jnp.logical_and(test, condition)

        for n in (0, 1):

            @pl.when(also(self.stays(n)))
            def _():
                pltpu.make_async_copy(block(n), slot(self.bit), self.local.at[0]).start()

            @pl.when(also(jnp.logical_not(self.stays(n))))
            def _():
                remote(
                    block(n), slot(self.bit), self.send.at[n], self.recv.at[self.bit], self.partners[n]
                ).start()

    def wait(self, block, slot):
        for n in (0, 1):

            @pl.when(self.stays(n))
            def _():
                pltpu.make_async_copy(block(n), slot(n), self.local.at[0]).wait()

            @pl.when(jnp.logical_not(self.stays(n)))
            def _():
                copy = remote(block(n), slot(n), self.send.at[n], self.recv.at[n], self.partners[n])
                copy.wait_send()
                copy.wait_recv()


SWAP_SCRATCH = [DMA((2,)), DMA((2,)), DMA((1,))]


def block_of(ref):
    return lambda n: ref.at[n]


def rows_block(ref):
    rows = ref.shape[0] // 2

    def view(n):
        start = n * rows if isinstance(n, int) else pl.multiple_of(n * rows, rows)
        return ref.at[pl.ds(start, rows)]

    return view


class Gather:
    def __init__(self, src, out, straight, copies, local):
        _, x_hi, z, core, y = place()
        self.right, self.left, self.across = (y + 1) % 4, (y + 3) % 4, (y + 2) % 4
        y_right, y_left = at_y(self.right), at_y(self.left)
        z_right, z_left = at_z(x_hi, (z + 1) % 4, core), at_z(x_hi, (z + 3) % 4, core)
        self.partners = [y_right, y_left, z_right, z_left]
        self.copies, self.local = copies, local
        self.src, self.out, self.y = src, out, y
        rows = (src.shape[0] - straight) // 4
        cut = rows // 32 * 16

        def at(start, count):
            return pl.ds(pl.multiple_of(start, 16), count)

        def ring(name, start, count, first_cut):
            own = src.at[at(start, count)]
            there = out.at[y, at(start, count)]
            copies.add(name + "r", own, there, y_right)
            copies.add(name + "l", own, there, y_left)
            one = out.at[self.left, at(start, first_cut)]
            two = out.at[self.right, at(start + first_cut, count - first_cut)]
            copies.add(name + "rr", one, one, y_right)
            copies.add(name + "ll", two, two, y_left)

        base = straight + z * rows
        ring("h", base, rows, cut)
        ring("s", 0, straight, straight // 32 * 16)
        for name, k in (("zl", self.left), ("zr", self.right), ("za", self.across)):
            own = out.at[k, at(base, rows)]
            copies.add(name + "r", own, own, z_right)
            copies.add(name + "l", own, own, z_left)
            one = out.at[k, at(straight + (z + 3) % 4 * rows, cut)]
            two = out.at[k, at(straight + (z + 1) % 4 * rows + cut, rows - cut)]
            copies.add(name + "rr", one, one, z_right)
            copies.add(name + "ll", two, two, z_left)

    def own(self):
        return pltpu.make_async_copy(self.src, self.out.at[self.y], self.local)

    def one(self):
        self.own().start()
        self.copies.start("hr", "hl")

    def two(self):
        c = self.copies
        c.arrive("hr")
        c.start("hrr", "zlr", "zll")
        c.arrive("hl")
        c.start("hll", "zrr", "zrl")
        c.start("sr", "sl")

    def three(self):
        c = self.copies
        c.arrive("hrr", "hll")
        c.start("zar", "zal")
        c.arrive("zlr")
        c.start("zlrr")
        c.arrive("zll")
        c.start("zlll")
        c.arrive("zrr")
        c.start("zrrr")
        c.arrive("zrl")
        c.start("zrll")

    def four(self):
        c = self.copies
        c.arrive("sr")
        c.start("srr")
        c.arrive("sl")
        c.start("sll")
        c.arrive("zar")
        c.start("zarr")
        c.arrive("zal")
        c.start("zall")

    def end(self):
        self.copies.arrive(
            "zlrr", "zlll", "zrrr", "zrll", "srr", "sll", "zarr", "zall"
        )
        self.copies.leave()
        self.own().wait()


GATHER_SCRATCH = [DMA((20,)), DMA((20,)), DMA((1,))]
MIX_STRAIGHT = 208
FEED_STRAIGHT = 256


def other_core(x_hi, z, core):
    return at_z(x_hi, z, 1 - core)


def inverse_rms(values):
    return lax.rsqrt(jnp.mean(values * values, axis=-1, keepdims=True) + norm_eps)


def my_rows(core, rows):
    return pl.ds(pl.multiple_of(core * rows, rows), rows)


def sigmoid(v):
    return 1.0 / (1.0 + jnp.exp(-v))


def softplus(v):
    return jnp.maximum(v, 0.0) + jnp.log1p(jnp.exp(-jnp.abs(v)))


def softplus_slope(value):
    near = value * (1.0 - 0.5 * value * (1.0 - value * (1.0 / 3.0)))
    return jnp.where(value < 0.01, near, 1.0 - jnp.exp(-value))


def iota(dims, axis):
    return lax.broadcasted_iota(jnp.int32, dims, axis)


def spread_heads(columns, rows):
    lane = iota((rows, LANES), 1)
    return jnp.where(
        lane < 64, columns[:, 0:1], jnp.where(lane < 128, columns[:, 1:2], columns[:, 2:3])
    )


def head_lanes(values, head):
    lane = iota(values.shape, 1)
    return jnp.where(jnp.logical_and(lane >= 64 * head, lane < 64 * head + 64), values, 0.0)


def in_lane(column, lane_at, rows):
    return jnp.where(iota((rows, 16), 1) == lane_at, column, 0.0)


def conv_taps(window, kernel):
    total = window[5 : 5 + CHUNK] * kernel[0:1]
    for k in range(1, 4):
        total = total + window[5 + k : 5 + k + CHUNK] * kernel[k : k + 1]
    return total


def masks_of(rows):
    return iota((rows, rows), 0) >= iota((rows, rows), 1)


def prepare_steps(normed_ref, step_rows, smalls, step_cols, dt_row, cum_row):
    raw = mm(normed_ref[...], jnp.concatenate([step_rows[k] for k in range(4)], axis=0), NT)

    def line(row):
        return jnp.concatenate([smalls[k, row : row + 1, 0:16] for k in range(4)], axis=1)

    dt = softplus(raw + line(4))
    a = -dt * jnp.exp(line(5))
    upto = masks_of(CHUNK).astype(f32)
    fill = jnp.zeros((CHUNK, 64), f32)
    for n in range(CHUNKS):
        at = pl.ds(n * CHUNK, CHUNK)
        dt_n = dt[n * CHUNK : (n + 1) * CHUNK]
        cum = mm(upto, a[n * CHUNK : (n + 1) * CHUNK], NN, HIGH)
        for k in range(4):
            own = slice(16 * k, 16 * k + 8)
            step_cols[k, at] = jnp.concatenate([dt_n[:, own], cum[:, own]], axis=1)
        both = jnp.concatenate([dt_n, cum], axis=1).T
        dt_row[:, at] = both[0:64]
        cum_row[:, at] = both[64:128]


def shared_forward(normed_ref, shared_ref, state_conv_ref, state_pad, b_ref, c_ref, b_turn):
    state_pad[0:8] = jnp.zeros((8, 256), f32)
    state_pad[pl.ds(8, 640)] = mm(normed_ref[...], shared_ref[0:256], NT)
    kernel = state_conv_ref[...]
    for n in range(CHUNKS):
        at = pl.ds(n * CHUNK, CHUNK)
        pre = conv_taps(state_pad[pl.ds(n * CHUNK, CHUNK + 8)], kernel)
        bc = pre * sigmoid(pre)
        b_ref[at] = bc[:, 0:128].astype(bf16)
        c_ref[at] = bc[:, 128:256].astype(bf16)
        b_turn[:, at] = bc[:, 0:128].T.astype(bf16)


def turn_into(out_ref, values):
    for n in range(CHUNKS):
        out_ref[:, pl.ds(n * CHUNK, CHUNK)] = (
            values[n * CHUNK : (n + 1) * CHUNK].astype(f32).T.astype(out_ref.dtype)
        )


def exchanged(rows):
    return jnp.concatenate([rows[32:64], rows[0:32]], axis=0)


def turned_heads(first, second, table_ref):
    return first * table_ref[:, 0:128] + second * table_ref[:, 128:256]


def keys_values(normed_ref, shared_ref, head, table_ref, key_ref, value_ref, value_turn):
    start = pl.multiple_of(head * 64, 64)
    key_rows = shared_ref[pl.ds(256 + start, 64)]
    value_rows = shared_ref[pl.ds(384 + start, 64)]
    rows = jnp.concatenate([value_rows, key_rows, value_rows, exchanged(key_rows)], axis=0)
    out = mm(normed_ref[...], rows, NT)
    key_ref[...] = turned_heads(out[:, 0:128], out[:, 128:256], table_ref).astype(bf16)
    values = jnp.where(iota((640, 128), 1) < 64, out[:, 0:128], 1.0)
    value_ref[...] = values.astype(bf16)
    turn_into(value_turn, values)


def mixer_rows(w):
    query_rows = w[384:448]
    return jnp.concatenate([w[0:192], query_rows, w[192:384], exchanged(query_rows)], axis=0)


QUERY_BLOCKS = ((0, 256), (256, 640))


def scores_of(key_ref, query_ref, first, last):
    scores = mm(key_ref[0:last], query_ref[first:last], NT)
    dims = scores.shape
    return jnp.where(iota(dims, 0) <= iota(dims, 1) + first, scores, -1e30)


def attend(query_ref, key_ref, value_turn, att):
    for first, last in QUERY_BLOCKS:
        scores = scores_of(key_ref, query_ref, first, last)
        top = jnp.max(scores, axis=0, keepdims=True)
        weights = jnp.exp(scores - top).astype(bf16)
        both = mm(value_turn[:, 0:last], weights, NN)
        out = both * (1.0 / both[64:65])
        for n in range(first // CHUNK, last // CHUNK):
            at = n * CHUNK - first
            att[pl.ds(n * CHUNK, CHUNK)] = out[:, at : at + CHUNK].T.astype(bf16)


def store_turned(out_ref, rows, values):
    for k in range(4):
        for x in range(2):
            out_ref[rows, pl.ds((2 * k + x) * 128, 128)] = values[
                :, (4 * x + k) * 128 : (4 * x + k + 1) * 128
            ].astype(bf16)


def silu_slope(pre, s):
    return s * (1.0 + pre * (1.0 - s))


def conv_back(after, kernel):
    total = after[3 : 3 + CHUNK] * kernel[0:1]
    for k in range(1, 4):
        total = total + after[3 - k : 3 - k + CHUNK] * kernel[k : k + 1]
    return total


def column_sum(values):
    return jnp.sum(values, axis=0, keepdims=True)


def attend_back(
    query_ref, key_ref, key_turn, value_ref, value_turn, grad_ref, att_turn, pairs_ref, key_grad, value_grad, table_ref
):
    for first, last in QUERY_BLOCKS:
        query = query_ref[first:last]
        grad = grad_ref[first:last]
        scores = scores_of(key_ref, query_ref, first, last)
        top = jnp.max(scores, axis=0, keepdims=True)
        weights = jnp.exp(scores - top)
        weights = weights * (1.0 / jnp.sum(weights, axis=0, keepdims=True))
        weights_low = weights.astype(bf16)
        att_turn[:, first:last] = mm(value_turn[0:64, 0:last], weights_low, NN).astype(bf16)
        slope = mm(value_ref[0:last], grad, NT)
        inner = jnp.sum(weights * slope, axis=0, keepdims=True)
        slope = (weights * (slope - inner)).astype(bf16)
        key_grad[0:last] += mm(slope, query, NN)
        value_grad[0:last] += mm(weights_low, grad, NN)
        query_grad = mm(key_turn[:, 0:last], slope, NN) * 0.125
        for n in range(first // CHUNK, last // CHUNK):
            at = pl.ds(n * CHUNK, CHUNK)
            turned = query_grad[:, n * CHUNK - first : (n + 1) * CHUNK - first].T
            pairs_ref[at, 192:256] = (turned * table_ref[at, 0:128]).astype(bf16)[:, 64:128]
            pairs_ref[at, 448:512] = (turned * table_ref[at, 128:256]).astype(bf16)[:, 64:128]


def rms_back(values, gain, grad):
    scale = inverse_rms(values)
    weighted = grad * gain
    unit = values * scale
    inner = jnp.mean(weighted * unit, axis=-1, keepdims=True)
    return scale * (weighted - unit * inner), jnp.sum(grad * unit, axis=0, keepdims=True)


REST = ROWS_OUT + ROWS_EXTRA
SMALL_ROWS = 80


def add_into(dst, sources, strip=None):
    if len(dst.shape) == 3:
        for k in range(dst.shape[0]):
            add_into(dst.at[k], [source.at[k] for source in sources], strip)
        return
    rows, width = dst.shape
    if strip is None:
        most = max(16, 65536 // width)
        strip = max(n for n in range(16, min(most, rows) + 1, 16) if rows % n == 0)

    def step(n, carry):
        at = pl.ds(pl.multiple_of(n * strip, 16), strip)
        total = sources[0][at].astype(f32)
        for source in sources[1:]:
            total = total + source[at].astype(f32)
        dst[at] = total.astype(dst.dtype)
        return carry

    lax.fori_loop(0, rows // strip, step, 0)


class RingSum:
    def __init__(self, name, copies, me, right, left, to_right, to_left, block, land, more=()):
        across = (me + 2) % 4
        self.name, self.copies, self.block, self.land = name, copies, block, land
        self.right, self.left, self.me = right, left, me
        copies.add(name + "a", block(across, 0), land(0, 0), to_right)
        copies.add(name + "b", block(across, 1), land(0, 1), to_left)
        copies.add(name + "c", land(0, 0), land(1, 0), to_right)
        copies.add(name + "d", land(0, 1), land(2, 1), to_left)
        copies.add(name + "e", block(right, 1), land(1, 1), to_right)
        copies.add(name + "f", block(left, 0), land(2, 0), to_left)

    def names(self, letters):
        return [self.name + letter for letter in letters]

    def start_far(self):
        self.copies.start(*self.names("ab"))

    def start_near(self):
        self.copies.start(*self.names("ef"))

    def start(self):
        self.start_far()
        self.start_near()

    def pass_on(self, mine_right, mine_left):
        for letter, mine, half, then in (("a", mine_right, 0, "c"), ("b", mine_left, 1, "d")):
            self.copies.arrive(self.name + letter)
            landed = self.land(0, half)
            add_into(landed, (mine, landed))
            self.copies.start(self.name + then)

    def arrive(self):
        self.copies.arrive(*self.names("efcd"))

    def drained(self):
        self.copies.left(*self.names("abef"))


def lanes_of(k, width):
    return pl.ds(pl.multiple_of(k * width, width), width)


def halves(rows, cut):
    return (pl.ds(0, cut), pl.ds(cut, rows - cut))


PAIRS = (pl.ds(0, 2), pl.ds(2, 2))
HALF_FEED = ROWS_FEED // 2
FEED_SUM = dict(
    sum_send=DMA((56,)),
    sum_recv=DMA((56,)),
    near_sem=DMA((6,)),
    land_py=VMEM((3, HALF_FEED, 1024), bf16),
    total_p=VMEM((HALF_FEED, 1024), bf16),
    land_pz=VMEM((3, HALF_FEED, 256), bf16),
    land_qz=VMEM((3, 4, HALF_FEED, 256), bf16),
    total_q=VMEM((4, HALF_FEED, 256), bf16),
    land_qy=VMEM((3, HALF_FEED, 256), bf16),
    feed_both=VMEM((ROWS_FEED, 256), bf16),
    land_x=VMEM((ROWS_FEED, 128), bf16),
    block=VMEM((3, ROWS_OUT, 1024), bf16),
    land_m=VMEM((4, 3, ROWS_OUT, 256), bf16),
    shared_sums=VMEM((4, ROWS_EXTRA, 1024), bf16),
    land_s=VMEM((3, 4, ROWS_EXTRA, 256), bf16),
)


class Sums:
    def __init__(self, r):
        _, x_hi, z, core, y = place()
        self.r, self.y, self.z, self.x_hi = r, y, z, x_hi
        self.y_right, self.y_left = (y + 1) % 4, (y + 3) % 4
        self.z_right, self.z_left = (z + 1) % 4, (z + 3) % 4
        to_y = at_y(self.y_right), at_y(self.y_left)
        to_z = at_z(x_hi, self.z_right, core), at_z(x_hi, self.z_left, core)
        x_other = at_z(1 - x_hi, z, core)
        self.partners = [*to_y, *to_z, x_other]
        self.copies = copies = Copies(r.sum_send, r.sum_recv)
        cut = halves(HALF_FEED, HALF_FEED // 2)
        self.cut = cut
        self.rest = pl.ds(HALF_FEED, HALF_FEED)

        def along_y(name, block, land):
            return RingSum(name, copies, y, self.y_right, self.y_left, *to_y, block, land)

        def along_z(name, block, land):
            return RingSum(name, copies, z, self.z_right, self.z_left, *to_z, block, land)

        self.py = along_y(
            "p", lambda k, n: r.feed.at[k, cut[n]], lambda slot, n: r.land_py.at[slot, cut[n]]
        )
        self.qz = along_z(
            "q",
            lambda k, n: r.feed.at[PAIRS[n], self.rest, lanes_of(k, 256)],
            lambda slot, n: r.land_qz.at[slot, PAIRS[n]],
        )
        self.pz = along_z(
            "u",
            lambda k, n: r.total_p.at[cut[n], lanes_of(k, 256)],
            lambda slot, n: r.land_pz.at[slot, cut[n]],
        )
        self.qy = along_y(
            "v", lambda k, n: r.total_q.at[k, cut[n]], lambda slot, n: r.land_qy.at[slot, cut[n]]
        )
        copies.add("x", r.feed_both.at[:, lanes_of(1 - x_hi, 128)], r.land_x, x_other)
        self.mix_cut = halves(ROWS_OUT, ROWS_OUT // 2)
        self.mix = [
            along_z(
                "abcd"[step],
                lambda k, n, step=step: r.block.at[step % 3, self.mix_cut[n], lanes_of(k, 256)],
                lambda slot, n, step=step: r.land_m.at[step, slot, self.mix_cut[n]],
            )
            for step in range(4)
        ]
        self.shared = along_z(
            "s",
            lambda k, n: r.shared_sums.at[PAIRS[n], :, lanes_of(k, 256)],
            lambda slot, n: r.land_s.at[slot, PAIRS[n]],
        )

    def fetches(self):
        r, feed, cut = self.r, self.r.feed, self.cut
        moves = (
            (feed.at[self.y_right, cut[0]], r.total_p.at[cut[0]]),
            (feed.at[self.y_left, cut[1]], r.total_p.at[cut[1]]),
            (feed.at[self.y, pl.ds(0, HALF_FEED)], r.total_p),
            (feed.at[PAIRS[0], self.rest, lanes_of(self.z_right, 256)], r.total_q.at[PAIRS[0]]),
            (feed.at[PAIRS[1], self.rest, lanes_of(self.z_left, 256)], r.total_q.at[PAIRS[1]]),
            (feed.at[:, self.rest, lanes_of(self.z, 256)], r.total_q),
        )
        return [
            pltpu.make_async_copy(src, dst, r.near_sem.at[n]) for n, (src, dst) in enumerate(moves)
        ]

    def feed_one(self):
        self.py.start_far()
        self.qz.start_far()
        for n in (0, 1, 3, 4):
            self.fetches()[n].start()

    def feed_two(self):
        r = self.r
        for n in (0, 1, 3, 4):
            self.fetches()[n].wait()
        self.py.pass_on(r.total_p.at[self.cut[0]], r.total_p.at[self.cut[1]])
        self.qz.pass_on(r.total_q.at[PAIRS[0]], r.total_q.at[PAIRS[1]])
        self.py.start_near()
        self.qz.start_near()
        for n in (2, 5):
            self.fetches()[n].start()

    def feed_three(self):
        r = self.r
        for n in (2, 5):
            self.fetches()[n].wait()
        self.py.arrive()
        add_into(r.total_p, (r.total_p, r.land_py.at[1], r.land_py.at[2]))
        self.pz.start()
        self.qz.arrive()
        add_into(r.total_q, (r.total_q, r.land_qz.at[1], r.land_qz.at[2]))
        self.qy.start()

    def feed_four(self):
        r, cut = self.r, self.cut
        self.pz.pass_on(
            r.total_p.at[cut[0], lanes_of(self.z_right, 256)],
            r.total_p.at[cut[1], lanes_of(self.z_left, 256)],
        )
        self.qy.pass_on(r.total_q.at[self.y_right, cut[0]], r.total_q.at[self.y_left, cut[1]])

    def feed_five(self):
        r = self.r
        self.pz.arrive()
        add_into(
            r.feed_both.at[pl.ds(0, HALF_FEED)],
            (r.total_p.at[:, lanes_of(self.z, 256)], r.land_pz.at[1], r.land_pz.at[2]),
        )
        self.qy.arrive()
        add_into(
            r.feed_both.at[self.rest], (r.total_q.at[self.y], r.land_qy.at[1], r.land_qy.at[2])
        )
        self.copies.start("x")

    def feed_six(self):
        r = self.r
        self.copies.arrive("x")
        add_into(r.feed_out, (r.feed_both.at[:, lanes_of(self.x_hi, 128)], r.land_x))

    def mix_pass(self, step):
        own = self.r.block.at[step % 3]
        self.mix[step].pass_on(
            own.at[self.mix_cut[0], lanes_of(self.z_right, 256)],
            own.at[self.mix_cut[1], lanes_of(self.z_left, 256)],
        )

    def mix_end(self, step):
        r = self.r
        self.mix[step].arrive()
        own = r.block.at[step % 3, :, lanes_of(self.z, 256)]
        add_into(
            r.sums.at[step, pl.ds(0, ROWS_OUT)], (own, r.land_m.at[step, 1], r.land_m.at[step, 2])
        )
        self.mix[step].drained()

    def shared_pass(self):
        own = self.r.shared_sums
        self.shared.pass_on(
            own.at[PAIRS[0], :, lanes_of(self.z_right, 256)],
            own.at[PAIRS[1], :, lanes_of(self.z_left, 256)],
        )

    def shared_end(self):
        r = self.r
        self.shared.arrive()
        add_into(
            r.sums.at[:, pl.ds(ROWS_OUT, ROWS_EXTRA)],
            (r.shared_sums.at[:, :, lanes_of(self.z, 256)], r.land_s.at[1], r.land_s.at[2]),
        )


def reduce_body(
    feed,
    sums,
    heads_ref,
    state_conv_ref,
    gain_one_ref,
    gain_two_ref,
    home_from,
    out_ref,
    shared_ref,
    small_out,
    home_ref,
    land_y,
    both,
    land_x,
    small_y,
    small_z,
    small_x,
    small_sum,
    send,
    recv,
    *swap_scratch,
):
    _, x_hi, z, core, y = place()
    right, left, across = (y + 1) % 4, (y + 3) % 4, (y + 2) % 4
    y_right, y_left, y_across = at_y(right), at_y(left), at_y(across)
    z_others = [at_z(x_hi, (z + n) % 4, core) for n in (1, 3, 2)]
    x_other = at_z(1 - x_hi, z, core)
    partner = other_core(x_hi, z, core)
    swap = Swap(*swap_scratch)
    copies = Copies(send, recv)
    cut = halves(REST, 432)
    ring = RingSum(
        "r",
        copies,
        y,
        right,
        left,
        y_right,
        y_left,
        lambda k, n: sums.at[k, cut[n]],
        lambda slot, n: land_y.at[slot, cut[n]],
    )
    mine = out_ref.at[core, pl.ds(0, ROWS_FEED)]
    copies.add("k2", mine, mine, partner)
    for n in range(2):
        copies.add(n, both.at[cut[n], lanes_of(1 - x_hi, 128)], land_x.at[cut[n]], x_other)
        mine = out_ref.at[core, pl.ds(ROWS_FEED + 432 * n, cut[n].size)]
        copies.add("k%d" % n, mine, mine, partner)
    for n, to in enumerate((y_right, y_left, y_across)):
        copies.add("sy%d" % n, small_sum.at[0], small_y.at[n], to)
        copies.add("sh%d" % n, shared_ref.at[y], shared_ref.at[y], to)
    for n, to in enumerate(z_others):
        copies.add("sz%d" % n, small_sum.at[1], small_z.at[n], to)
    copies.add("sx", small_sum.at[2], small_x.at[0], x_other)
    copies.add("small", small_out.at[core], small_out.at[core], partner)

    swap.greet([y_right, y_left, y_across, *z_others, x_other, partner])
    ring.start()
    out_ref[core, pl.ds(0, ROWS_FEED)] = feed[...]
    copies.start("k2")
    for k in range(4):
        small_sum[0, pl.ds(16 * k, 16)] = heads_ref[k]
        small_sum[0, 68 + k : 69 + k] = gain_one_ref[:, 256 * k : 256 * k + 256]
        small_sum[0, 72 + k : 73 + k] = gain_two_ref[:, 256 * k : 256 * k + 256]
    small_sum[0, 64:68] = state_conv_ref[...]
    small_sum[0, 76:80] = jnp.zeros((4, 256), f32)
    copies.start("sy0", "sy1", "sy2")
    ring.pass_on(sums.at[right, cut[0]], sums.at[left, cut[1]])
    swap.start(rows_block(home_from), block_of(home_ref))
    copies.arrive("sy0", "sy1", "sy2")
    small_sum[1] = small_sum[0] + small_y[0] + small_y[1] + small_y[2]
    copies.start("sz0", "sz1", "sz2")
    copies.arrive("sz0", "sz1", "sz2")
    small_sum[2] = small_sum[1] + small_z[0] + small_z[1] + small_z[2]
    copies.start("sx")
    copies.arrive("sx")
    small_out[core] = small_sum[2] + small_x[0]
    copies.start("small")
    for n, letters in enumerate(("fc", "ed")):
        copies.arrive(*ring.names(letters))
        add_into(
            both.at[cut[n]], (sums.at[y, cut[n]], land_y.at[1, cut[n]], land_y.at[2, cut[n]])
        )
        copies.start(n)
    for n in range(2):
        copies.arrive(n)
        own = both.at[cut[n], lanes_of(x_hi, 128)]
        add_into(out_ref.at[core, pl.ds(ROWS_FEED + 432 * n, cut[n].size)], (own, land_x.at[cut[n]]))
        copies.start("k%d" % n)
    copies.arrive("k0", "k1", "k2")
    shared_at = pl.ds(ROWS_FEED + ROWS_OUT, ROWS_SHARED)
    shared_ref[y] = out_ref[0, shared_at] + out_ref[1, shared_at]
    copies.start("sh0", "sh1", "sh2")
    swap.wait(rows_block(home_from), block_of(home_ref))
    copies.arrive("small", "sh0", "sh1", "sh2")
    copies.leave()


def reduce_grads(feed, sums, heads, state_conv, gain_one, gain_two, home, collective):
    small = (SMALL_ROWS, 256)
    rows, width = home.shape
    return kernel_call(
        reduce_body,
        "reduce_grads",
        collective,
        [
            shape((2, ROWS_ALL, 128), f32),
            shape((4, ROWS_SHARED, 128), f32),
            shape((2,) + small, f32),
            shape((2, rows // 2, width), bf16),
        ],
        (feed, sums, heads, state_conv, gain_one, gain_two, home),
        [
            VMEM((3, REST, 256), bf16),
            VMEM((REST, 256), bf16),
            VMEM((REST, 128), bf16),
            VMEM((3,) + small, f32),
            VMEM((3,) + small, f32),
            VMEM((1,) + small, f32),
            VMEM((3,) + small, f32),
            DMA((24,)),
            DMA((24,)),
        ]
        + SWAP_SCRATCH,
    )


def whole(dims):
    return pl.BlockSpec(dims, lambda y: (0,) * len(dims), pipeline_mode=pl.Buffered(1))


def by_step(dims):
    return pl.BlockSpec((1,) + tuple(dims[1:]), lambda y: (y,) + (0,) * (len(dims) - 1))


STEP_ROWS = pl.BlockSpec((4, 16, 1024), lambda y: (0, 28, 0))
ANYWHERE = pl.BlockSpec(memory_space=ANY)


def staged(body, name, collective, inputs, outputs, scratch, steps=4):
    names = [*inputs, *outputs, *scratch]

    def kernel(*refs):
        body(types.SimpleNamespace(**dict(zip(names, refs))))

    results = pl.pallas_call(
        kernel,
        name=name,
        grid=(steps,),
        in_specs=[spec or whole(array.shape) for array, spec in inputs.values()],
        out_specs=[spec or whole(dims) for dims, _, spec in outputs.values()],
        out_shape=[shape(dims, kind) for dims, kind, _ in outputs.values()],
        scratch_shapes=list(scratch.values()),
        compiler_params=pltpu.CompilerParams(
            dimension_semantics=("arbitrary",),
            vmem_limit_bytes=60 * 2**20,
            collective_id=collective,
            has_side_effects=collective is not None,
        ),
    )(*[array for array, _ in inputs.values()])
    return types.SimpleNamespace(**dict(zip(outputs, results)))


def hail(partners):
    barrier = pltpu.get_barrier_semaphore()
    for partner in partners:
        pl.semaphore_signal(barrier, inc=1, device_id=partner, device_id_type=MESH)


def hailed(count):
    pl.semaphore_wait(pltpu.get_barrier_semaphore(), count)


PAIR_SCRATCH = dict(
    acc=VMEM((640, 1024), f32),
    part=VMEM((320, 1024), bf16),
    land=VMEM((320, 1024), bf16),
    pair_send=DMA((5,)),
    pair_recv=DMA((5,)),
)
PIECES = ((0, 160), (160, 160))


class Pair:
    def __init__(self, r):
        _, x_hi, z, core, _ = place()
        self.r, self.core = r, core
        self.partner = other_core(x_hi, z, core)
        self.copies = Copies(r.pair_send, r.pair_recv)
        for n, piece in enumerate(PIECES):
            self.copies.add("p%d" % n, r.part.at[pl.ds(*piece)], r.land.at[pl.ds(*piece)], self.partner)

    def rows(self, mine, start=0, count=320):
        side = self.core if mine else 1 - self.core
        return pl.ds(pl.multiple_of(side * 320 + start, 16), count)

    def add_gather(self, full):
        for n, piece in enumerate(PIECES):
            there = full.at[self.rows(True, *piece)]
            self.copies.add("g%d" % n, there, there, self.partner)

    def close(self, last):
        r = self.r
        theirs = self.rows(False)
        r.part[...] = (r.acc[theirs] + last(theirs)).astype(bf16)
        self.copies.start("p0", "p1")
        own = self.rows(True)
        r.acc[own] += last(own)

    def total(self, n):
        self.copies.arrive("p%d" % n)
        start, count = PIECES[n]
        return self.r.acc[self.rows(True, start, count)] + self.r.land[pl.ds(start, count)].astype(f32)


def add_step(y, acc, total):
    @pl.when(y == 0)
    def _():
        acc[...] = total()

    @pl.when(jnp.logical_and(y > 0, y < 3))
    def _():
        acc[...] += total()


def normed_rows(values, gain):
    return (values * inverse_rms(values) * gain).astype(bf16)


MIX_SCRATCH = dict(
    x_pad=VMEM((648, LANES), f32),
    z_part=VMEM((640, LANES), f32),
    step_cols=VMEM((4, 640, 16), f32),
    dt_row=VMEM((64, 640), f32),
    cum_row=VMEM((64, 640), f32),
    query=VMEM((640, 128), bf16),
    gated=VMEM((640, LANES), bf16),
    state_pad=VMEM((648, 256), f32),
    b=VMEM((640, 128), bf16),
    c=VMEM((640, 128), bf16),
    b_turn=VMEM((128, 640), bf16),
    key=VMEM((640, 128), bf16),
    value=VMEM((640, 128), bf16),
    value_turn=VMEM((128, 640), bf16),
    state=VMEM((128, LANES), f32),
)


def mixer_start(y, normed, r):
    @pl.when(y == 0)
    def _():
        shared_forward(normed, r.shared, r.state_conv, r.state_pad, r.b, r.c, r.b_turn)
        prepare_steps(normed, r.step_rows, r.small, r.step_cols, r.dt_row, r.cum_row)
        r.x_pad[0:8] = jnp.zeros((8, LANES), f32)

    @pl.when(y % 2 == 0)
    def _():
        keys_values(normed, r.shared, y // 2, r.table, r.key, r.value, r.value_turn)

    proj = mm(normed[...], mixer_rows(r.w.at[0]), NT)
    r.z_part[...] = proj[:, 0:192]
    r.x_pad[pl.ds(8, 640)] = proj[:, 256:448]
    query = turned_heads(proj[:, 128:256], proj[:, 384:512], r.table)
    r.query[...] = (query * 0.125).astype(bf16)


def scan(y, r):
    small = r.small[y]
    skip = spread_heads(small[6:7, 0:16], 1)
    causal = masks_of(CHUNK)
    kernel = small[0:4, 0:LANES]
    own_rows = pl.ds(pl.multiple_of(16 * y, 16), 16)
    r.state[...] = jnp.zeros((128, LANES), f32)
    for n in range(CHUNKS):
        at = pl.ds(n * CHUNK, CHUNK)
        pre = conv_taps(r.x_pad[pl.ds(n * CHUNK, CHUNK + 8)], kernel)
        u = pre * sigmoid(pre)
        dt = r.step_cols[y, at]
        cum = pltpu.roll(dt, 8, 1)
        dt_r = r.dt_row[own_rows, at]
        cum_r = r.cum_row[own_rows, at]
        c_chunk = r.c[at]
        inter = mm(c_chunk, r.b[at], NT)
        mixing = []
        inputs = []
        for h in range(3):
            gap = cum[:, h : h + 1] - cum_r[h : h + 1]
            decay = jnp.exp(jnp.where(causal, gap, -1e30))
            mixing.append((inter * decay * dt_r[h : h + 1]).astype(bf16))
            inputs.append(head_lanes(u, h).astype(bf16))
        inside = mm(jnp.concatenate(mixing, axis=1), jnp.concatenate(inputs, axis=0), NN)
        old = r.state[...]
        low = old.astype(bf16)
        if hasattr(r, "states"):
            r.states[0, n] = low
        before = mm(c_chunk, low, NN) * spread_heads(jnp.exp(cum), CHUNK)
        out = inside + before + skip * u
        z = r.z_part[at]
        r.gated[at] = (out * (z * sigmoid(z))).astype(bf16)
        end = cum[CHUNK - 1 : CHUNK]
        feed = spread_heads(dt * jnp.exp(end - cum), CHUNK) * u
        r.state[...] = old * spread_heads(jnp.exp(end), 1) + mm(r.b_turn[:, at], feed.astype(bf16), NN)


def middle_end(pair, hidden, r):
    for n, (start, count) in enumerate(PIECES):
        piece = pl.ds(start, count)
        middle = hidden[piece].astype(f32) + pair.total(n)
        r.middle[piece] = middle
        r.full[pair.rows(True, start, count)] = normed_rows(middle, r.gain_two[...])
        pair.copies.start("g%d" % n)
    pair.copies.arrive("g0", "g1")
    pair.copies.leave()
    r.normed_two[...] = r.full[...]


def mix_steps(y, pair, normed, hidden, r):
    mixer_start(y, normed, r)
    attend(r.query, r.key, r.value_turn, r.att)
    scan(y, r)
    w = r.w.at[0]

    def share(rows):
        return mm(r.gated[rows], w[464:656], NN) + mm(r.att[rows, 0:64], w[656:720], NN)

    add_step(y, r.acc, lambda: share(pl.ds(0, 640)))

    @pl.when(y == 3)
    def _():
        pair.close(share)
        middle_end(pair, hidden, r)


def mix_first_body(r):
    y = pl.program_id(0)
    pair = Pair(r)
    pair.add_gather(r.full)
    gather = Gather(r.feed, r.feed_all, FEED_STRAIGHT, Copies(r.send, r.recv), r.local.at[0])

    @pl.when(y == 0)
    def _():
        greet(gather.partners + [pair.partner])
        gather.one()

    for n, stage in enumerate((gather.two, gather.three, gather.four)):

        @pl.when(y == n + 1)
        def _():
            stage()

    mix_steps(y, pair, r.normed, r.hidden, r)

    @pl.when(y == 3)
    def _():
        gather.end()


def mix_second_body(r):
    y = pl.program_id(0)
    section = lax.axis_index(SECTION)
    pair = Pair(r)
    pair.add_gather(r.full)
    mine = r.normed_full.at[pair.rows(True)]
    pair.copies.add("n", mine, mine, pair.partner)

    @pl.when(y == 0)
    def _():
        hail([pair.partner])

        @pl.when(section == 0)
        def _():
            r.hidden[...] = r.own[...]

        @pl.when(section == 1)
        def _():
            r.hidden[...] = r.received[...]

        r.normed_full[pair.rows(True)] = normed_rows(r.hidden[...].astype(f32), r.gain_one[...])
        hailed(1)
        pair.copies.start("n")
        pair.copies.arrive("n")

    mix_steps(y, pair, r.normed_full, r.hidden, r)

    @pl.when(y == 3)
    def _():
        r.normed[...] = r.normed_full[...]


def mixer_inputs(w_mix, small, shared, state_conv, table):
    return dict(
        w=(w_mix, by_step(w_mix.shape)),
        step_rows=(w_mix, STEP_ROWS),
        small=(small, None),
        shared=(shared, None),
        state_conv=(state_conv, None),
        table=(table, None),
    )


MIDDLE_OUT = dict(middle=((320, 1024), f32, None), normed_two=((640, 1024), bf16, None))
FULL = dict(full=VMEM((640, 1024), bf16))


def mix_first(normed, hidden, mixer, gain_two, feed, collective):
    return staged(
        mix_first_body,
        "mix_first",
        collective,
        dict(normed=(normed, None), hidden=(hidden, None), gain_two=(gain_two, None), feed=(feed, None))
        | mixer_inputs(*mixer),
        MIDDLE_OUT | dict(feed_all=((4,) + feed.shape, bf16, ANYWHERE)),
        PAIR_SCRATCH
        | MIX_SCRATCH
        | FULL
        | dict(att=VMEM((640, 128), bf16), send=DMA((20,)), recv=DMA((20,)), local=DMA((1,))),
    )


def mix_second(own, received, mixer, gain_one, gain_two, collective):
    return staged(
        mix_second_body,
        "mix_second",
        collective,
        dict(
            own=(own, None),
            received=(received, None),
            gain_one=(gain_one, None),
            gain_two=(gain_two, None),
        )
        | mixer_inputs(*mixer),
        MIDDLE_OUT
        | dict(
            normed=((640, 1024), bf16, None),
            hidden=((320, 1024), bf16, None),
            states=((4, CHUNKS, 128, LANES), bf16, by_step((4, CHUNKS, 128, LANES))),
        ),
        PAIR_SCRATCH
        | MIX_SCRATCH
        | FULL
        | dict(att=VMEM((640, 128), bf16), normed_full=VMEM((640, 1024), bf16)),
    )


def feed_body(r, further):
    y = pl.program_id(0)
    section = lax.axis_index(SECTION)
    pair = Pair(r)
    beyond = {SECTION: 1 - section}
    if further:
        for n, piece in enumerate(PIECES):
            piece = pl.ds(*piece)
            pair.copies.add("s%d" % n, r.low.at[piece], r.beyond.at[piece], beyond)

    @pl.when(y == 0)
    def _():
        hail([pair.partner] + ([beyond] if further else []))

    w = r.w.at[0]
    both = mm(r.normed_two[...], w[0:512], NT)
    gate, up = both[:, 0:256], both[:, 256:512]
    r.active[...] = (gate * sigmoid(gate) * up).astype(bf16)

    def share(rows):
        return mm(r.active[rows], w[512:768], NN)

    add_step(y, r.acc, lambda: share(pl.ds(0, 640)))

    @pl.when(y == 3)
    def _():
        hailed(2 if further else 1)
        pair.close(share)
        for n, piece in enumerate(PIECES):
            piece = pl.ds(*piece)
            low = (r.middle[piece] + pair.total(n)).astype(bf16)
            if further:
                r.low[piece] = low
                pair.copies.start("s%d" % n)
            else:
                r.out[piece] = low
        if further:
            pair.copies.arrive("s0", "s1")
            r.out[...] = r.beyond[...]
        pair.copies.leave()


def feed_layer(normed_two, w_feed, middle, collective, further):
    more = dict(low=VMEM((320, 1024), bf16), beyond=VMEM((320, 1024), bf16)) if further else {}
    return staged(
        functools.partial(feed_body, further=further),
        "feed_first" if further else "feed_second",
        collective,
        dict(normed_two=(normed_two, None), middle=(middle, None), w=(w_feed, by_step(w_feed.shape))),
        dict(out=((320, 1024), bf16, None)),
        PAIR_SCRATCH | dict(active=VMEM((640, 256), bf16)) | more,
    ).out


def feed_back_body(r):
    y = pl.program_id(0)
    weights_too = hasattr(r, "sums")
    section = lax.axis_index(SECTION)
    pair = Pair(r)
    pair.add_gather(r.full)
    mine = r.grad_full.at[pair.rows(True)]
    pair.copies.add("n", mine, mine, pair.partner)

    @pl.when(y == 0)
    def _():
        hail([pair.partner])

        @pl.when(section == 0)
        def _():
            r.grad_full[pair.rows(True)] = r.received[...]

        @pl.when(section == 1)
        def _():
            r.grad_full[pair.rows(True)] = r.own[...]

        hailed(1)
        pair.copies.start("n")
        pair.copies.arrive("n")

    w = r.w.at[0]
    both = mm(r.normed_two[...], w[0:512], NT)
    gate, up = both[:, 0:256], both[:, 256:512]
    act_grad = mm(r.grad_full[...], w[512:768], NT)
    s = sigmoid(gate)
    silu = gate * s
    r.gate_grad[:, 0:256] = (act_grad * up * silu_slope(gate, s)).astype(bf16)
    r.gate_grad[:, 256:512] = (act_grad * silu).astype(bf16)
    if weights_too:
        out = r.sums.at[0]
        store_turned(out, pl.ds(512, 256), mm((silu * up).astype(bf16), r.grad_full[...], TN))
        store_turned(out, pl.ds(0, 512), mm(r.gate_grad[...], r.normed_two[...], TN))

    def share(rows):
        return mm(r.gate_grad[rows], w[0:512], NN)

    add_step(y, r.acc, lambda: share(pl.ds(0, 640)))

    @pl.when(y == 3)
    def _():
        pair.close(share)
        gain_sum = jnp.zeros((1, 1024), f32)
        for n, (start, count) in enumerate(PIECES):
            piece = pl.ds(start, count)
            back, gain_grad = rms_back(r.middle[piece], r.gain_two[...], pair.total(n))
            gain_sum = gain_sum + gain_grad
            rows = pair.rows(True, start, count)
            total = r.grad_full[rows].astype(f32) + back
            r.middle_grad[piece] = total
            r.full[rows] = total.astype(bf16)
            pair.copies.start("g%d" % n)
        if weights_too:
            r.gain_grad[...] = gain_sum
        pair.copies.arrive("g0", "g1")
        pair.copies.leave()
        r.branch_grad[...] = r.full[...]


def feed_back(own, received, normed_two, middle, w_feed, gain_two, collective, weights_too):
    more = {}
    if weights_too:
        more = dict(
            sums=((4, ROWS_FEED, 1024), bf16, by_step((4, ROWS_FEED, 1024))),
            gain_grad=((1, 1024), f32, None),
        )
    return staged(
        feed_back_body,
        "feed_back_sums" if weights_too else "feed_back",
        collective,
        dict(
            own=(own, None),
            received=(received, None),
            normed_two=(normed_two, None),
            middle=(middle, None),
            gain_two=(gain_two, None),
            w=(w_feed, by_step(w_feed.shape)),
        ),
        dict(middle_grad=((320, 1024), f32, None), branch_grad=((640, 1024), bf16, None)) | more,
        PAIR_SCRATCH | FULL | dict(grad_full=VMEM((640, 1024), bf16), gate_grad=VMEM((640, 512), bf16)),
    )


MIX_BACK_SCRATCH = dict(
    att_turn=VMEM((64, 640), bf16),
    c_turn=VMEM((128, 640), bf16),
    key_turn=VMEM((128, 640), bf16),
    gated_grad=VMEM((640, LANES), f32),
    att_grad=VMEM((640, 128), bf16),
    proj_grad=VMEM((640, 512), bf16),
    key_grad=VMEM((640, 128), f32),
    value_grad=VMEM((640, 128), f32),
    keyval_grad=VMEM((640, 256), bf16),
    pre_grad=VMEM((648, LANES), f32),
    line_grad=VMEM((128, 640), f32),
    step_slopes=VMEM((4, 640, 16), f32),
    end_grad=VMEM((4, 8, 16), f32),
    step_grad=VMEM((640, 64), bf16),
    inter_grad=VMEM((CHUNKS, CHUNK, CHUNK), f32),
    b_grad=VMEM((640, 128), f32),
    c_grad=VMEM((640, 128), f32),
    bc_pre_grad=VMEM((648, 256), f32),
    bc_grad=VMEM((640, 256), bf16),
)


def scan_back(y, r, weights_too):
    small = r.small[y]
    kernel = small[0:4, 0:LANES]
    skip = spread_heads(small[6:7, 0:16], 1)
    own_rows = pl.ds(pl.multiple_of(16 * y, 16), 16)
    r.state[...] = jnp.zeros((128, LANES), f32)
    skip_sum = jnp.zeros((1, LANES), f32)
    kernel_sum = [jnp.zeros((1, LANES), f32) for _ in range(4)]
    causal = masks_of(CHUNK)
    follows = iota((CHUNK, CHUNK), 0) <= iota((CHUNK, CHUNK), 1)
    for n in range(CHUNKS - 1, -1, -1):
        at = pl.ds(n * CHUNK, CHUNK)
        window = r.x_pad[pl.ds(n * CHUNK, CHUNK + 8)]
        pre = conv_taps(window, kernel)
        s = sigmoid(pre)
        u = pre * s
        dt = r.step_cols[y, at]
        cum = pltpu.roll(dt, 8, 1)
        dt_r = r.dt_row[own_rows, at]
        cum_r = r.cum_row[own_rows, at]
        b_chunk = r.b[at]
        c_chunk = r.c[at]
        inter = mm(c_chunk, b_chunk, NT)
        inter_t = mm(b_chunk, c_chunk, NT)
        end = cum[CHUNK - 1 : CHUNK]
        start_state = r.states[0, n]
        reach = spread_heads(jnp.exp(cum), CHUNK)
        before = mm(c_chunk, start_state, NN) * reach
        z = r.z_part[at]
        sz = sigmoid(z)
        silu_z = z * sz
        out_grad = r.gated_grad[at]
        y_grad = out_grad * silu_z
        u_low = u.astype(bf16)
        mixing = []
        mixing_t = []
        inputs = []
        grads = []
        dt_grad = jnp.zeros((CHUNK, 16), f32)
        cum_grad = jnp.zeros((CHUNK, 16), f32)
        lines_dt = []
        lines_cum = []
        inter_total = r.inter_grad[n]
        for h in range(3):
            gap = cum[:, h : h + 1] - cum_r[h : h + 1]
            decay = jnp.exp(jnp.where(causal, gap, -1e30))
            gap_t = cum_r[h : h + 1] - cum[:, h : h + 1]
            decay_t = jnp.exp(jnp.where(follows, gap_t, -1e30))
            weight = decay * dt_r[h : h + 1]
            mixing.append((inter * weight).astype(bf16))
            mixing_t.append((inter_t * decay_t * dt[:, h : h + 1]).astype(bf16))
            inputs.append(head_lanes(u, h).astype(bf16))
            own = head_lanes(y_grad, h).astype(bf16)
            grads.append(own)
            mix_grad = mm(own, u_low, NT)
            inter_total = inter_total + mix_grad * weight
            per = mix_grad * inter * decay
            column = column_sum(per)
            lines_dt.append(column)
            lines_cum.append(-dt_r[h : h + 1] * column)
            row_sum = jnp.sum(per * dt_r[h : h + 1], axis=1, keepdims=True)
            cum_grad = cum_grad + in_lane(row_sum, 8 + h, CHUNK)
        r.inter_grad[n] = inter_total
        inside = mm(jnp.concatenate(mixing, axis=1), jnp.concatenate(inputs, axis=0), NN)
        out = inside + before + skip * u
        r.gated[at] = (out * silu_z).astype(bf16)
        r.proj_grad[at, 0:192] = (out_grad * out * silu_slope(z, sz)).astype(bf16)
        u_grad = mm(jnp.concatenate(mixing_t, axis=1), jnp.concatenate(grads, axis=0), NN)
        u_grad = u_grad + skip * y_grad
        if weights_too:
            skip_sum = skip_sum + column_sum(y_grad * u)
        reached = (y_grad * reach).astype(bf16)
        later = r.state[...]
        later_low = later.astype(bf16)
        left = jnp.exp(end - cum)
        fed = dt * left
        fed_wide = spread_heads(fed, CHUNK)
        r.c_grad[at] += mm(reached, start_state, NT)
        r.b_grad[at] += mm((fed_wide * u).astype(bf16), later_low, NT)
        from_state = mm(b_chunk, later_low, NN)
        u_grad = u_grad + fed_wide * from_state
        before_grad = y_grad * before
        fed_grad = u * from_state
        state_share = column_sum(later * start_state.astype(f32)) * spread_heads(jnp.exp(end), 1)
        end_grad = jnp.zeros((1, 16), f32)
        for h in range(3):
            cum_grad = cum_grad + in_lane(
                jnp.sum(head_lanes(before_grad, h), axis=1, keepdims=True), 8 + h, CHUNK
            )
            fed_h = jnp.sum(head_lanes(fed_grad, h), axis=1, keepdims=True)
            dt_grad = dt_grad + in_lane(fed_h * left[:, h : h + 1], h, CHUNK)
            moved = fed_h * fed[:, h : h + 1]
            cum_grad = cum_grad - in_lane(moved, 8 + h, CHUNK)
            share = jnp.sum(head_lanes(state_share, h), axis=1, keepdims=True)
            end_grad = end_grad + in_lane(column_sum(moved) + share, h, 1)
        r.state[...] = later * spread_heads(jnp.exp(end), 1) + mm(r.c_turn[:, at], reached, NN)
        rest = jnp.zeros((5, CHUNK), f32)
        first = pl.ds(pl.multiple_of(16 * y, 16), 8)
        second = pl.ds(pl.multiple_of(64 + 16 * y, 16), 8)
        r.line_grad[first, at] = jnp.concatenate(lines_dt + [rest], axis=0)
        r.line_grad[second, at] = jnp.concatenate(lines_cum + [rest], axis=0)
        r.step_slopes[y, at] = dt_grad + cum_grad
        r.end_grad[y, n : n + 1] = end_grad
        own_pre = u_grad * silu_slope(pre, s)
        r.pre_grad[at] = own_pre
        after = r.pre_grad[pl.ds(n * CHUNK, CHUNK + 8)]
        r.proj_grad[at, 256:448] = conv_back(after, kernel).astype(bf16)
        if weights_too:
            for k in range(4):
                kernel_sum[k] = kernel_sum[k] + column_sum(own_pre * window[5 + k : 5 + k + CHUNK])
    if weights_too:
        skip_row = jnp.zeros((1, 16), f32)
        for h in range(3):
            skip_row = skip_row + in_lane(
                jnp.sum(head_lanes(skip_sum, h), axis=1, keepdims=True), h, 1
            )
        grads = r.small_grad.at[y]
        grads[...] = jnp.zeros((16, 256), f32)
        for k in range(4):
            grads[k : k + 1, 0:LANES] = kernel_sum[k]
        grads[6:7, 0:16] = skip_row


def steps_back(r, weights_too):
    def wide(ref, at):
        return jnp.concatenate([ref[k, at] for k in range(4)], axis=1)

    rate = jnp.exp(jnp.concatenate([r.small[k, 5:6, 0:16] for k in range(4)], axis=1))
    follows = (iota((CHUNK, CHUNK), 0) <= iota((CHUNK, CHUNK), 1)).astype(f32)
    bias_sum = jnp.zeros((1, 64), f32)
    decay_sum = jnp.zeros((1, 64), f32)
    for n in range(CHUNKS):
        at = pl.ds(n * CHUNK, CHUNK)
        turned = r.line_grad[:, at].T
        dt = wide(r.step_cols, at)
        slopes = [r.step_slopes[k, at] for k in range(4)]
        low = iota((CHUNK, 16), 1) < 8
        dt_own = [jnp.where(low, own, 0.0) for own in slopes]
        cum_own = [jnp.where(low, pltpu.roll(own, 8, 1), 0.0) for own in slopes]
        cum_grad = jnp.concatenate(cum_own, axis=1) + turned[:, 64:128]
        a_grad = mm(follows, cum_grad, NN, HIGH) + wide(r.end_grad, pl.ds(n, 1))
        dt_grad = jnp.concatenate(dt_own, axis=1) + turned[:, 0:64] - rate * a_grad
        raw_grad = dt_grad * softplus_slope(dt)
        r.step_grad[at] = raw_grad.astype(bf16)
        bias_sum = bias_sum + column_sum(raw_grad)
        decay_sum = decay_sum - column_sum(a_grad * dt) * rate
    if weights_too:
        for k in range(4):
            r.small_grad[k, 4:5, 0:16] = bias_sum[:, 16 * k : 16 * k + 16]
            r.small_grad[k, 5:6, 0:16] = decay_sum[:, 16 * k : 16 * k + 16]


def shared_back(r, weights_too):
    sums = [jnp.zeros((1, 256), f32) for _ in range(4)]
    kernel = r.state_conv[...]
    for n in range(CHUNKS - 1, -1, -1):
        at = pl.ds(n * CHUNK, CHUNK)
        inter_low = r.inter_grad[n].astype(bf16)
        grad_b = r.b_grad[at] + mm(inter_low, r.c[at], TN)
        grad_c = r.c_grad[at] + mm(inter_low, r.b[at], NN)
        window = r.state_pad[pl.ds(n * CHUNK, CHUNK + 8)]
        pre = conv_taps(window, kernel)
        own_pre = jnp.concatenate([grad_b, grad_c], axis=1) * silu_slope(pre, sigmoid(pre))
        r.bc_pre_grad[at] = own_pre
        after = r.bc_pre_grad[pl.ds(n * CHUNK, CHUNK + 8)]
        r.bc_grad[at] = conv_back(after, kernel).astype(bf16)
        if weights_too:
            for k in range(4):
                sums[k] = sums[k] + column_sum(own_pre * window[5 + k : 5 + k + CHUNK])
    if weights_too:
        for k in range(4):
            r.state_conv_grad[k : k + 1] = sums[k]


def mix_back_body(r):
    y = pl.program_id(0)
    weights_too = hasattr(r, "sums")
    section = lax.axis_index(SECTION)
    pair = Pair(r)
    beyond = {SECTION: 1 - section}
    if weights_too:
        sums = Sums(r)

        @pl.when(y == 0)
        def _():
            greet(sums.partners + [pair.partner])
            sums.feed_one()

        @pl.when(y == 1)
        def _():
            sums.feed_two()
            sums.mix[0].start()

        @pl.when(y == 2)
        def _():
            sums.feed_three()
            sums.mix_pass(0)
            sums.mix[1].start()

        @pl.when(y == 3)
        def _():
            sums.feed_four()
            sums.mix_end(0)
            sums.mix_pass(1)
            sums.mix[2].start()

    else:
        swap = Swap(r.swap_send, r.swap_recv, r.swap_local)
        for n, piece in enumerate(PIECES):
            piece = pl.ds(*piece)
            pair.copies.add("s%d" % n, r.low.at[piece], r.beyond.at[piece], beyond)

        @pl.when(y == 0)
        def _():
            swap.greet([pair.partner, beyond])
            swap.start(rows_block(r.result), block_of(r.home_land))

    mixer_start(y, r.normed, r)

    @pl.when(y == 0)
    def _():
        turn_into(r.c_turn, r.c[...])
        r.pre_grad[pl.ds(640, 8)] = jnp.zeros((8, LANES), f32)
        r.bc_pre_grad[pl.ds(640, 8)] = jnp.zeros((8, 256), f32)
        r.inter_grad[...] = jnp.zeros((CHUNKS, CHUNK, CHUNK), f32)
        r.b_grad[...] = jnp.zeros((640, 128), f32)
        r.c_grad[...] = jnp.zeros((640, 128), f32)
        r.line_grad[...] = jnp.zeros((128, 640), f32)

    @pl.when(y % 2 == 0)
    def _():
        turn_into(r.key_turn, r.key[...])
        r.key_grad[...] = jnp.zeros((640, 128), f32)
        r.value_grad[...] = jnp.zeros((640, 128), f32)

    w = r.w.at[0]
    nothing = jnp.zeros((64, 1024), bf16)
    branch_rows = jnp.concatenate([w[464:656], nothing, w[656:720], nothing], axis=0)
    branch = mm(r.branch_grad[...], branch_rows, NT)
    r.gated_grad[...] = branch[:, 0:192]
    r.att_grad[...] = branch[:, 256:384].astype(bf16)
    attend_back(
        r.query,
        r.key,
        r.key_turn,
        r.value,
        r.value_turn,
        r.att_grad,
        r.att_turn,
        r.proj_grad,
        r.key_grad,
        r.value_grad,
        r.table,
    )
    scan_back(y, r, weights_too)

    def share(at):
        return mm(r.proj_grad[at], mixer_rows(r.w.at[0]), NN)

    add_step(y, r.acc, lambda: share(pl.ds(0, 640)))
    for head in range(2):

        @pl.when(y == 2 * head + 1)
        def _():
            own = r.key_grad[...]
            first = jnp.where(
                iota((640, 128), 1) < 64, r.value_grad[...], own * r.table[:, 0:128]
            )
            second = own * r.table[:, 128:256]
            r.keyval_grad[...] = jnp.concatenate([first, second], axis=1).astype(bf16)

    def keyval_rows(head):
        key_rows = r.shared[pl.ds(256 + 64 * head, 64)]
        value_rows = r.shared[pl.ds(384 + 64 * head, 64)]
        return jnp.concatenate([value_rows, key_rows, value_rows, exchanged(key_rows)], axis=0)

    @pl.when(y == 1)
    def _():
        r.acc[...] += mm(r.keyval_grad[...], keyval_rows(0), NN)

    @pl.when(y == 3)
    def _():
        shared_back(r, weights_too)
        steps_back(r, weights_too)

    if weights_too:
        out = r.block.at[y % 3]
        normed = r.normed[...]
        grad = r.branch_grad[...]
        own = mm(r.proj_grad[...], normed, TN)
        store_turned(out, pl.ds(0, 192), own[0:192])
        store_turned(out, pl.ds(192, 192), own[256:448])
        store_turned(out, pl.ds(384, 64), own[192:256] + exchanged(own[448:512]))
        store_turned(out, pl.ds(448, 192), mm(r.gated[...], grad, TN))
        store_turned(out, pl.ds(640, 64), mm(r.att_turn[...], grad, NN))
        for head in range(2):

            @pl.when(y == 2 * head + 1)
            def _():
                own = mm(r.keyval_grad[...], normed, TN)
                at = pl.ds(64 * head, 64)
                store_turned(r.shared_sums.at[2], at, own[64:128] + exchanged(own[192:256]))
                store_turned(r.shared_sums.at[3], at, own[0:64])

        @pl.when(y == 3)
        def _():
            both = mm(r.bc_grad[...], normed, TN)
            store_turned(r.shared_sums.at[0], pl.ds(0, 128), both[0:128])
            store_turned(r.shared_sums.at[1], pl.ds(0, 128), both[128:256])
            steps = mm(r.step_grad[...], normed, TN)
            for k in range(4):
                store_turned(r.shared_sums.at[k], pl.ds(128, 16), steps[16 * k : 16 * k + 16])
            sums.mix[3].start()
            sums.shared.start()

    @pl.when(y == 3)
    def _():
        step_weights = jnp.concatenate([r.step_rows[k] for k in range(4)], axis=0)

        def last(at):
            return (
                share(at)
                + mm(r.keyval_grad[at], keyval_rows(1), NN)
                + mm(r.bc_grad[at], r.shared[0:256], NN)
                + mm(r.step_grad[at], step_weights, NN)
            )

        pair.close(last)
        if weights_too:
            sums.feed_five()
            sums.mix_end(1)
            sums.mix_pass(2)
            sums.mix_pass(3)
            sums.shared_pass()
        gain_sum = jnp.zeros((1, 1024), f32)
        for n, (start, count) in enumerate(PIECES):
            piece = pl.ds(start, count)
            hidden = r.hidden[piece].astype(f32)
            back, gain_grad = rms_back(hidden, r.gain_one[...], pair.total(n))
            low = (r.middle_grad[piece] + back).astype(bf16)
            gain_sum = gain_sum + gain_grad
            if weights_too:
                r.grad_in[piece] = low
            else:
                r.low[piece] = low
                pair.copies.start("s%d" % n)
        if weights_too:
            r.gain_grad[...] = gain_sum
            sums.feed_six()
            sums.mix_end(2)
            sums.mix_end(3)
            sums.shared_end()
            sums.copies.leave()
        else:
            swap.wait(rows_block(r.result), block_of(r.home_land))
            r.home[...] = r.home_land[...]
            pair.copies.arrive("s0", "s1")
            r.received[...] = r.beyond[...]
        pair.copies.leave()


def mix_back(forward, branch_grad, middle_grad, mixer, gain_one, collective, result=None, feed=None):
    inputs = dict(
        normed=(forward.normed, None),
        hidden=(forward.hidden, None),
        states=(forward.states, by_step(forward.states.shape)),
        branch_grad=(branch_grad, None),
        middle_grad=(middle_grad, None),
        gain_one=(gain_one, None),
    ) | mixer_inputs(*mixer)
    scratch = PAIR_SCRATCH | MIX_SCRATCH | MIX_BACK_SCRATCH
    if feed is None:
        inputs |= dict(result=(result, None))
        outputs = dict(received=((320, 1024), bf16, None), home=((2, 160, 1024), bf16, None))
        scratch = scratch | dict(
            low=VMEM((320, 1024), bf16),
            beyond=VMEM((320, 1024), bf16),
            home_land=VMEM((2, 160, 1024), bf16),
            swap_send=DMA((2,)),
            swap_recv=DMA((2,)),
            swap_local=DMA((1,)),
        )
    else:
        inputs |= dict(feed=(feed, ANYWHERE))
        outputs = dict(
            grad_in=((320, 1024), bf16, None),
            gain_grad=((1, 1024), f32, None),
            sums=((4, ROWS_OUT + ROWS_EXTRA, 256), bf16, None),
            small_grad=((4, 16, 256), f32, None),
            state_conv_grad=((4, 256), f32, None),
            feed_out=((ROWS_FEED, 128), f32, None),
        )
        scratch = scratch | FEED_SUM
    return staged(
        mix_back_body,
        "mix_back" if feed is None else "mix_back_sums",
        collective,
        inputs,
        outputs,
        scratch,
    )


def pick(rows, columns, start):
    return (iota((rows, columns), 1) == iota((rows, columns), 0) + start).astype(bf16)


def write_turn_table(table_ref):
    lane = iota((640, 128), 1)
    pair = (lane % 32).astype(f32)
    frequency = jnp.exp(pair * (-2.0 / 64.0 * math.log(rope_base)))
    angle = iota((640, 128), 0).astype(f32) * frequency
    kept = lane >= 64
    sine = jnp.sin(angle)
    table_ref[:, 0:128] = jnp.where(kept, jnp.cos(angle), 0.0)
    table_ref[:, 128:256] = jnp.where(kept, jnp.where(lane < 96, -sine, sine), 0.0)


def start_body(r):
    section, x_hi, z, core, y = place()
    gather = Gather(r.mix, r.mix_all, MIX_STRAIGHT, Copies(r.send, r.recv), r.local.at[0])
    swap = Swap(r.swap_send, r.swap_recv, r.swap_local)
    small = Copies(r.small_send, r.small_recv)
    for n, k in enumerate((gather.right, gather.left, gather.across)):
        small.add(n, r.small, r.small_land.at[y], at_y(k))
    partner = other_core(x_hi, z, core)
    mine = r.normed_full.at[my_rows(core, 320)]
    small.add(3, mine, mine, partner)

    def turned(values, rows, start):
        return mm(pick(rows, values.shape[1], start), values, NT).astype(bf16)

    swap.greet(gather.partners + [at_y(gather.across), partner])
    swap.start(block_of(r.stream), rows_block(r.own_land), section == 0)
    swap.start(block_of(r.cotangent), rows_block(r.own_land), section == 1)
    r.mix[464:656] = r.mamba_out[pl.ds(pl.multiple_of(core * 192, 192), 192)]
    r.mix[656:720] = r.att_out[pl.ds(pl.multiple_of(core * 64, 64), 64)]
    r.mix[0:192] = turned(r.mamba[:, 0:384], 192, core * 192)
    r.mix[192:384] = turned(r.mamba[:, 384:768], 192, core * 192)
    r.mix[384:448] = turned(r.query[...], 64, core * 64)
    wanted = jnp.logical_and(
        iota((16, 128), 1) == iota((16, 128), 0) + core * 3, iota((16, 128), 0) < 3
    )
    r.mix[448:464] = mm(wanted.astype(bf16), r.step[...], NT).astype(bf16)
    gather.one()
    small.start(0, 1, 2)
    r.small_land[y] = r.small[...]
    r.shared[0:256] = turned(r.state[...], 256, 0)
    r.shared[256:512] = turned(r.keyval[...], 256, 0)
    gather.two()
    swap.wait(block_of(r.stream), rows_block(r.own_land))
    r.own[...] = r.own_land[...]
    r.normed_full[my_rows(core, 320)] = normed_rows(r.own[...].astype(f32), r.gain_one[...])
    small.start(3)
    r.feed[0:256] = turned(r.gate_up[:, 0:512], 256, core * 256)
    r.feed[256:512] = turned(r.gate_up[:, 512:1024], 256, core * 256)
    r.feed[512:768] = r.down[pl.ds(pl.multiple_of(core * 256, 256), 256)]
    gather.three()
    write_turn_table(r.table)
    gather.four()
    small.arrive(0, 1, 2, 3)
    small.leave()
    r.small_all[...] = r.small_land[...]
    r.normed[...] = r.normed_full[...]
    gather.end()


def start(inputs, collective):
    rows = 320
    return staged(
        start_body,
        "start",
        collective,
        {name: (array, None) for name, array in inputs.items()},
        dict(
            mix_all=((4, ROWS_MIX, 1024), bf16, ANYWHERE),
            feed=((ROWS_FEED, 1024), bf16, None),
            shared=((512, 1024), bf16, None),
            small_all=((4, 16, 256), f32, None),
            own=((rows, 1024), bf16, None),
            normed=((2 * rows, 1024), bf16, None),
            table=((640, 256), f32, None),
        ),
        dict(
            mix=VMEM((ROWS_MIX, 1024), bf16),
            small_land=VMEM((4, 16, 256), f32),
            own_land=VMEM((rows, 1024), bf16),
            normed_full=VMEM((2 * rows, 1024), bf16),
            send=DMA((20,)),
            recv=DMA((20,)),
            local=DMA((1,)),
            small_send=DMA((4,)),
            small_recv=DMA((4,)),
            swap_send=DMA((2,)),
            swap_recv=DMA((2,)),
            swap_local=DMA((1,)),
        ),
        steps=1,
    )


def chosen(rows, start, width=128):
    return (iota((rows, width), 1) == iota((rows, width), 0) + start).astype(f32)


def finish_body(r):
    _, x_hi, z, core, y = place()
    own = chosen(64, core * 64)
    f = ROWS_FEED

    def across(side, start, stop):
        return mm(own, r.sums[side, start:stop], NT, HIGH)

    def along(side, start, stop):
        return mm(r.sums[side, start:stop], own, NT, HIGH)

    for c in range(2):
        for n in range(2):
            r.mamba_in[:, n, 192 * c : 192 * c + 192] = across(c, f + 192 * n, f + 192 * n + 192)
            r.gate_up[:, n, 256 * c : 256 * c + 256] = across(c, 256 * n, 256 * n + 256)
        r.query_in[:, 64 * c : 64 * c + 64] = across(c, f + 384, f + 448)
        r.step_in[:, 3 * c : 3 * c + 3] = across(c, f + 832, f + 848)[:, 0:3]
        r.mamba_out[192 * c : 192 * c + 192] = along(c, f + 448, f + 640)
        r.attention_out[64 * c : 64 * c + 64] = along(c, f + 640, f + 704)
        r.down_weight[256 * c : 256 * c + 256] = along(c, 512, 768)
        heads = r.small[c, pl.ds(pl.multiple_of(16 * y, 16), 16)]
        r.mamba_conv[:, 192 * c : 192 * c + 192] = heads[0:4, 0:192]
        r.step_bias[:, 3 * c : 3 * c + 3] = heads[4:5, 0:3]
        r.decay_log[:, 3 * c : 3 * c + 3] = heads[5:6, 0:3]
        r.skip_gain[:, 3 * c : 3 * c + 3] = heads[6:7, 0:3]
    few = chosen(16, core * 64 + y * 16)
    shared = [mm(few, r.shared_sums[k], NT, HIGH) for k in range(4)]
    for k in range(2):
        r.state_in[:, 128 * k : 128 * k + 128] = shared[k]
        r.keyval_in[:, k] = shared[2 + k]
    tiny = (x_hi * 8 + z * 2 + core) * 4 + y
    kernel = r.small[0, 64:68] + r.small[1, 64:68]
    r.state_conv[...] = mm(kernel, chosen(4, tiny * 4, 256), NT, HIGH)
    lanes = chosen(16, tiny % 16 * 16, 256)
    for out, start in ((r.mixer_gain, 68), (r.feed_gain, 72)):
        both = r.small[0, start : start + 4] + r.small[1, start : start + 4]
        row = jnp.sum(jnp.where(iota((4, 256), 0) == tiny // 16, both, 0.0), axis=0, keepdims=True)
        out[...] = mm(row, lanes, NT, HIGH)
    r.section_output[...] = r.result[...].astype(f32)
    r.input_grad[...] = r.grad[...].astype(f32)


def finish(sums, shared_sums, small, result, grad):
    inputs = dict(sums=sums, shared_sums=shared_sums, small=small, result=result, grad=grad)
    outputs = dict(
        section_output=(2, 160, 1024),
        input_grad=(2, 160, 1024),
        mixer_gain=(1, 16),
        mamba_in=(64, 2, 384),
        state_in=(16, 256),
        step_in=(64, 6),
        mamba_conv=(4, 384),
        state_conv=(4, 4),
        step_bias=(1, 6),
        decay_log=(1, 6),
        skip_gain=(1, 6),
        query_in=(64, 128),
        keyval_in=(16, 2, 128),
        mamba_out=(384, 64),
        attention_out=(128, 64),
        feed_gain=(1, 16),
        gate_up=(64, 2, 512),
        down_weight=(512, 64),
    )
    return staged(
        finish_body,
        "finish",
        None,
        {name: (array, None) for name, array in inputs.items()},
        {name: (dims, f32, None) for name, dims in outputs.items()},
        {},
        steps=1,
    )


def per_device(
    stream_in,
    cotangent,
    mixer_gain,
    mamba_in,
    state_in,
    step_in,
    mamba_conv,
    state_conv,
    step_bias,
    decay_log,
    skip_gain,
    query_in,
    keyval_in,
    mamba_out,
    attention_out,
    feed_gain,
    gate_up,
    down_weight,
):
    core = lax.axis_index(DP) % 2
    gain_one = mixer_gain.astype(f32)
    gain_two = feed_gain.astype(f32)

    def mine(values, axis):
        size = values.shape[axis] // 2
        return lax.dynamic_slice_in_dim(values, core * size, size, axis)

    conv_mine = jnp.pad(mine(mamba_conv[0].astype(f32), 1), ((0, 0), (0, 64)))
    heads_mine = jnp.stack([mine(step_bias[0], 0), mine(decay_log[0], 0), mine(skip_gain[0], 0)])
    small_mine = jnp.concatenate(
        [
            conv_mine,
            jnp.pad(heads_mine, ((0, 1), (0, 253))),
            jnp.pad(heads_mine.T, ((0, 5), (0, 253))),
        ]
    )
    begun = start(
        dict(
            mamba=mamba_in[0].reshape(1024, 768),
            query=query_in[0],
            step=jnp.pad(step_in[0], ((0, 0), (0, 122))),
            mamba_out=mamba_out[0],
            att_out=attention_out[0],
            gate_up=gate_up[0].reshape(1024, 1024),
            down=down_weight[0],
            state=state_in[0],
            keyval=keyval_in[0].reshape(1024, 256),
            small=small_mine,
            stream=stream_in,
            cotangent=cotangent,
            gain_one=gain_one,
        ),
        1,
    )
    own = begun.own
    mixer = (begun.mix_all, begun.small_all, begun.shared, state_conv[0].astype(f32), begun.table)

    first = mix_first(begun.normed, own, mixer, gain_two, begun.feed, 4)
    w_feed = first.feed_all
    received = feed_layer(first.normed_two, w_feed, first.middle, 5, True)
    forward = mix_second(own, received, mixer, gain_one, gain_two, 6)
    result = feed_layer(forward.normed_two, w_feed, forward.middle, 7, False)
    back = feed_back(own, own, forward.normed_two, forward.middle, w_feed, gain_two, 8, False)
    moved = mix_back(forward, back.branch_grad, back.middle_grad, mixer, gain_one, 9, result=result)
    back = feed_back(own, moved.received, forward.normed_two, forward.middle, w_feed, gain_two, 10, True)
    ends = mix_back(forward, back.branch_grad, back.middle_grad, mixer, gain_one, 11, feed=back.sums)
    reduced, shared_sum, small_sum, input_grad = reduce_grads(
        ends.feed_out,
        ends.sums,
        ends.small_grad,
        ends.state_conv_grad,
        ends.gain_grad,
        back.gain_grad,
        ends.grad_in,
        12,
    )
    done = finish(reduced, shared_sum, small_sum, moved.home, input_grad)
    return tuple(value.reshape(1, *value.shape[value.shape[0] == 1 :]) for value in vars(done).values())


def solution(mesh):
    in_specs = (
        P(DP, TENSOR, None),
        P(DP, TENSOR, None),
        P(SECTION, None),
        P(SECTION, None, None, TENSOR),
        P(SECTION, None, None),
        P(SECTION, None, TENSOR),
        P(SECTION, None, TENSOR),
        P(SECTION, None, None),
        P(SECTION, TENSOR),
        P(SECTION, TENSOR),
        P(SECTION, TENSOR),
        P(SECTION, None, TENSOR),
        P(SECTION, None, None, None),
        P(SECTION, TENSOR, None),
        P(SECTION, TENSOR, None),
        P(SECTION, None),
        P(SECTION, None, None, TENSOR),
        P(SECTION, TENSOR, None),
    )
    out_specs = (
        P(SECTION, DP, TENSOR, None),
        P(SECTION, DP, TENSOR, None),
        P(SECTION, (DP, TENSOR)),
        P(SECTION, DP, None, TENSOR),
        P(SECTION, (DP, TENSOR), None),
        P(SECTION, DP, TENSOR),
        P(SECTION, None, TENSOR),
        P(SECTION, None, (DP, TENSOR)),
        P(SECTION, TENSOR),
        P(SECTION, TENSOR),
        P(SECTION, TENSOR),
        P(SECTION, DP, TENSOR),
        P(SECTION, (DP, TENSOR), None, None),
        P(SECTION, TENSOR, DP),
        P(SECTION, TENSOR, DP),
        P(SECTION, (DP, TENSOR)),
        P(SECTION, DP, None, TENSOR),
        P(SECTION, TENSOR, DP),
    )
    return jax.shard_map(
        per_device, mesh=mesh, in_specs=in_specs, out_specs=out_specs, check_vma=False
    )
```
